512 devices in a mesh: dp: 16 (over y_hi, x, core), ctx: 8 (over z), mp: 4 (over y_lo).
Axes of the slice: x: 4, y: 8 (y_hi: 2, y_lo: 4; y = y_hi * 4 + y_lo), z: 8, core: 2. Of those that a mesh axis runs over, the one named last changes fastest.
Arguments:
- queries: bfloat16 [24576, 4096], P(('dp', 'ctx'), 'mp'), may hold values from -96 to 96
- key_states: bfloat16 [24576, 512], P(('dp', 'ctx'), 'mp'), may hold values from -12 to 12
- normed: bfloat16 [24576, 8192], P(('dp', 'ctx'), 'mp'), may hold values from -24 to 24
- value_weight: bfloat16 [8192, 512], P(('dp', 'ctx'), 'mp'), may hold values from -0.0625 to 0.0625
- grad_out: bfloat16 [24576, 4096], P(('dp', 'ctx'), 'mp'), may hold values from -6 to 6
- lengths: int32 [16, 8], P('dp'), may hold values from 1 to 768, 1536 in all within a row
Outputs:
- attended: bfloat16 [24576, 4096], P(('dp', 'ctx'), 'mp')
- grad_query: bfloat16 [24576, 4096], P(('dp', 'ctx'), 'mp')
- grad_key: bfloat16 [24576, 512], P(('dp', 'ctx'), 'mp')
- grad_weight: float32 [8192, 512], P(('dp', 'ctx'), 'mp')
The draws below stay inside these ranges and needn't reach their ends.
Inputs may be any that keep to these rules, and one draw needn't show every extreme that they name: Each row holds the lengths of one pack's documents and sums to 1536; the longest is exactly 768.
All inputs are finite; a program needn't handle non-finite values.
Results may differ from the reference program's by a relative error of at most 0.04.
Values may be sent and summed in bfloat16 or wider, within the bound.
No kernel may reach another device: no remote copies, remote signals or barrier semaphores. Data moves between devices by JAX's collectives and lax.ppermute only.
A program may use at most 64 MiB of HBM per device.

```python
import math
import jax
import jax.numpy as jnp
import numpy as np
from jax import lax

D = 8192
HEADS = 32
KV_HEADS = 4
HEAD_DIM = 128
NDOC = 8
PACK = 1536
TOKENS = 24576
N_DP = 16


def make_keys(key):
    draws = jnp.clip(jax.random.normal(key, (TOKENS, KV_HEADS * HEAD_DIM), jnp.float32), -4.0, 4.0)
    spread = jnp.exp(jax.random.uniform(jax.random.fold_in(key, 5), (TOKENS, 1), jnp.float32, jnp.log(0.3), jnp.log(3.0)))
    scaled = draws * spread
    tied = scaled
    return tied


def draw_key_states(key, part):
    tied = make_keys(key)
    return tied.astype(jnp.bfloat16)


def draw_queries(key, part):
    key = jax.random.fold_in(key, 3)
    spread = jnp.exp(jax.random.uniform(jax.random.fold_in(key, 1), (TOKENS, 1), jnp.float32, jnp.log(0.3), jnp.log(3.0)))
    draws = jnp.clip(jax.random.normal(key, (TOKENS, HEADS * HEAD_DIM), jnp.float32), -4.0, 4.0)
    query_rows = draws * spread
    return jnp.clip(query_rows, -96.0, 96.0).astype(jnp.bfloat16)


def raised(values, key, source, target, shards_of, factor):
    owner, partner = [(jnp.arange(values.shape[position]) // (values.shape[position] // shards_of)).reshape([-1 if axis == position else 1 for axis in range(values.ndim)]) for position in (source, target)]
    chosen = jax.random.permutation(key, shards_of)[partner]
    strong = (owner == chosen) | (owner == (partner + shards_of // 2) % shards_of)
    return jnp.where(strong, factor * values, values)


def level_of(rng, dims, split, least, high):
    gain, own = 1.0, jax.random.fold_in(rng, 6)
    for dim, shards_of in split:
        steps = jnp.exp(jax.random.uniform(jax.random.fold_in(own, dim), (shards_of,), jnp.float32, least / len(split), high / len(split)))
        gain = gain * jnp.repeat(steps, dims[dim] // shards_of).reshape([-1 if axis == dim else 1 for axis in range(len(dims))])
    return gain


def length_profile(number_of, total, limit, slope):
    portions = [(1 << 20) // math.isqrt(grade ** slope) + 1 for grade in range(2, number_of + 1)]
    rest, counts = total - limit - (number_of - 1), [1] * (number_of - 1)
    while rest > 0:
        movable = [i for i in range(number_of - 1) if counts[i] < limit]
        pool, left = sum([portions[i] for i in movable]), rest
        for i in movable:
            addition = min(limit - counts[i], max(1, left * portions[i] // pool), rest)
            counts[i] = counts[i] + addition
            rest = rest - addition
    return np.array([limit] + counts)


def uneven(key, amount, total, limit, lean):
    if amount == 2:
        one = jax.random.randint(key, (), max(1, total - limit), min(limit, total - 1) + 1)
        return jnp.stack([one, total - one])
    sizes = jnp.asarray(length_profile(amount, total, limit, lean), jnp.int32)
    twos = (amount - 1) // 2
    donor, sink = sizes[1:1 + 2 * twos:2], sizes[2:2 + 2 * twos:2]
    slack = jnp.minimum(donor - 1, limit - sink)
    moved = jax.random.randint(jax.random.fold_in(key, 1), (twos,), 0, 1 << 20) % (slack + 1)
    sizes = sizes.at[1:1 + 2 * twos:2].set(donor - moved).at[2:2 + 2 * twos:2].set(sink + moved)
    return sizes[jax.random.permutation(jax.random.fold_in(key, 2), amount)]


def gaussian(stream_key, dims, width, most, cuts=(), kind=jnp.bfloat16):
    entries = width * jax.random.normal(stream_key, dims, jnp.float32)
    if cuts:
        entries = entries * level_of(stream_key, dims, cuts, -0.22, 0.18)
    return jnp.clip(entries, -most, most).astype(kind)


def gaussian_with(key, shape, scale, limit, cuts, heavy, held_as=jnp.bfloat16):
    result = scale * jax.random.normal(key, shape, jnp.float32)
    if cuts:
        result = result * level_of(key, shape, cuts, -0.22, 0.18)
    return jnp.clip(raised(result, jax.random.fold_in(key, 3), *heavy), -limit, limit).astype(held_as)


def setup_inputs(seed: int = 0) -> dict:
    streams_of = jax.random.split(jax.random.key(seed), 7)
    queries = draw_queries(jax.random.fold_in(streams_of[6], 71), 0)
    key_states = draw_key_states(jax.random.fold_in(streams_of[6], 71), 0)
    normed = gaussian_with(streams_of[2], (TOKENS, D), 1.0, 24.0, ((0, 128), (1, 4)), (0, 1, 128, 5.5))
    value_weight = gaussian(streams_of[3], (D, KV_HEADS * HEAD_DIM), D ** -0.5, 0.0625, ((0, 128), (1, 4)))
    grad_out = gaussian(streams_of[4], (TOKENS, HEADS * HEAD_DIM), 1.0, 6.0, ((0, 128), (1, 4)))
    lengths = jax.vmap(lambda own: uneven(own, NDOC, PACK, PACK // 2, 2))(jax.random.split(streams_of[5], N_DP)).reshape((N_DP, NDOC)).astype(jnp.int32)
    return {"queries": queries, "key_states": key_states, "normed": normed, "value_weight": value_weight, "grad_out": grad_out, "lengths": lengths}


def attend(query_head, key_head, value_head, grad_head, allowed):
    score_scale = HEAD_DIM ** -0.5
    highest = lax.Precision.HIGHEST
    query_float = query_head.astype(jnp.float32)
    key_float = key_head.astype(jnp.float32)
    value_float = value_head.astype(jnp.float32)
    grad_float = grad_head.astype(jnp.float32)
    visible = allowed[:, None, :]
    scores = jnp.einsum("tgd,jd->tgj", query_float, key_float, precision=highest) * score_scale
    masked = jnp.where(visible, scores, -jnp.inf)
    row_max = jnp.max(masked, axis=-1, keepdims=True)
    log_total = row_max + jnp.log(jnp.sum(jnp.exp(masked - row_max), axis=-1, keepdims=True))
    attn_probs = jnp.where(visible, jnp.exp(scores - log_total), jnp.float32(0.0))
    attended = jnp.einsum("tgj,jd->tgd", attn_probs, value_float, precision=highest).astype(jnp.bfloat16)
    row_dots = jnp.sum(grad_float * attended.astype(jnp.float32), axis=-1)
    grad_probs = jnp.einsum("tgd,jd->tgj", grad_float, value_float, precision=highest)
    grad_scores = (attn_probs * (grad_probs - row_dots[..., None])).astype(jnp.bfloat16)
    grad_scores = lax.optimization_barrier(grad_scores).astype(jnp.float32)
    probs_half = lax.optimization_barrier(attn_probs.astype(jnp.bfloat16)).astype(jnp.float32)
    grad_value = jnp.einsum("tgj,tgd->jd", probs_half, grad_float, precision=highest).astype(jnp.bfloat16)
    grad_key = (jnp.einsum("tgj,tgd->jd", grad_scores, query_float, precision=highest) * score_scale).astype(jnp.bfloat16)
    grad_query = (jnp.einsum("tgj,jd->tgd", grad_scores, key_float, precision=highest) * score_scale).astype(jnp.bfloat16)
    return attended, grad_query, grad_key, grad_value


def reference(queries, key_states, normed, value_weight, grad_out, lengths):
    kv_group = HEADS // KV_HEADS
    projected = jnp.dot(normed, value_weight, preferred_element_type=jnp.float32).astype(jnp.bfloat16)
    query_packs = queries.reshape(N_DP, PACK, KV_HEADS, kv_group, HEAD_DIM).transpose(0, 2, 1, 3, 4)
    grad_packs = grad_out.reshape(N_DP, PACK, KV_HEADS, kv_group, HEAD_DIM).transpose(0, 2, 1, 3, 4)
    key_packs = key_states.reshape(N_DP, PACK, KV_HEADS, HEAD_DIM).transpose(0, 2, 1, 3)
    value_packs = projected.reshape(N_DP, PACK, KV_HEADS, HEAD_DIM).transpose(0, 2, 1, 3)
    positions = jnp.arange(PACK, dtype=jnp.int32)

    def one_pack(inputs):
        query_pack, key_pack, value_pack, grad_pack, doc_lengths = inputs
        doc_ends = jnp.cumsum(doc_lengths).astype(jnp.int32)
        documents = jnp.sum((positions[:, None] >= doc_ends[None, :]).astype(jnp.int32), axis=1)
        allowed = (documents[:, None] == documents[None, :]) & (positions[None, :] <= positions[:, None])
        return lax.map(lambda head_set: attend(head_set[0], head_set[1], head_set[2], head_set[3], allowed),
                       (query_pack, key_pack, value_pack, grad_pack))

    attended, grad_query, grad_key, grad_value = lax.map(
        one_pack, (query_packs, key_packs, value_packs, grad_packs, lengths))
    attended = attended.transpose(0, 2, 1, 3, 4).reshape(TOKENS, HEADS * HEAD_DIM)
    grad_query = grad_query.transpose(0, 2, 1, 3, 4).reshape(TOKENS, HEADS * HEAD_DIM)
    grad_key = grad_key.transpose(0, 2, 1, 3).reshape(TOKENS, KV_HEADS * HEAD_DIM)
    grad_value = grad_value.transpose(0, 2, 1, 3).reshape(TOKENS, KV_HEADS * HEAD_DIM)
    grad_weight = lax.dot_general(normed, grad_value, (((0,), (0,)), ((), ())), preferred_element_type=jnp.float32)
    return attended, grad_query, grad_key, grad_weight
```

```python
import functools

import jax
import jax.numpy as jnp
from jax import lax
from jax.experimental import pallas as pl
from jax.experimental.pallas import tpu as pltpu
from jax.sharding import Mesh, PartitionSpec as P

HEAD_DIM = 128
TOK = 192
GROUP = 8
WINDOW = 5 * TOK
PACK = 8 * TOK
HEADS_AT_ONCE = 2
LANES = HEADS_AT_ONCE * TOK
CHIPS = ("yh", "x", "ctx")
PAIR_MP = ("core", "mp")
F32 = jnp.float32
BF16 = jnp.bfloat16


def swapped_with_mp(block):
    route = []
    for yh in range(2):
        for x in range(4):
            for mp in range(4):
                source = (yh * 4 + x) * 4 + mp
                target = ((mp >> 1) * 4 + (mp & 1) * 2 + (x & 1)) * 4 + yh * 2 + (x >> 1)
                route.append((source, target))
    return lax.ppermute(block, ("yh", "x", "mp"), route)


def to_all(block, axes, copies):
    return lax.all_to_all(
        jnp.broadcast_to(block[None], (copies,) + block.shape), axes, 0, 0, tiled=True
    )


def project_kernel(x_ref, other_ref, w_ref, out_ref):
    core = lax.axis_index("core")
    weight = jnp.concatenate(
        [w_ref[c].reshape(1024, HEAD_DIM) for c in range(4)], axis=1
    )
    own = jnp.concatenate(
        [x_ref[:, pl.ds(pl.multiple_of((2 * part + core) * 512, 512), 512)] for part in range(2)],
        axis=1,
    )
    for rows, place in ((own, core), (other_ref[...], 1 - core)):
        result = jnp.dot(rows, weight, preferred_element_type=F32)
        for c in range(4):
            out_ref[place * 4 + c] = result[:, c * HEAD_DIM : (c + 1) * HEAD_DIM].astype(BF16)


def project(x, other, weight):
    return pl.pallas_call(
        project_kernel,
        out_shape=jax.ShapeDtypeStruct((8, TOK, HEAD_DIM), BF16),
        in_specs=[pl.BlockSpec(memory_space=pltpu.VMEM)] * 3,
        out_specs=pl.BlockSpec(memory_space=pltpu.VMEM),
        compiler_params=pltpu.CompilerParams(vmem_limit_bytes=48 * 2**20),
        name="project",
    )(x, other, weight)


def weight_grad_kernel(x_ref, other_ref, dv_ref, out_ref):
    core = lax.axis_index("core")
    own_dv = jnp.concatenate([dv_ref[core * 4 + c] for c in range(4)], axis=1)
    other_dv = jnp.concatenate([dv_ref[(1 - core) * 4 + c] for c in range(4)], axis=1)
    contract = (((0,), (0,)), ((), ()))
    for part in range(2):
        own = x_ref[:, pl.ds(pl.multiple_of((2 * part + core) * 512, 512), 512)]
        other = other_ref[:, part * 512 : (part + 1) * 512]
        result = lax.dot_general(own, own_dv, contract, preferred_element_type=F32)
        result += lax.dot_general(other, other_dv, contract, preferred_element_type=F32)
        for c in range(4):
            out_ref[c, part] = result[:, c * HEAD_DIM : (c + 1) * HEAD_DIM].astype(BF16)


def weight_grad(x, other, dv):
    return pl.pallas_call(
        weight_grad_kernel,
        out_shape=jax.ShapeDtypeStruct((4, 2, 512, HEAD_DIM), BF16),
        in_specs=[pl.BlockSpec(memory_space=pltpu.VMEM)] * 3,
        out_specs=pl.BlockSpec(memory_space=pltpu.VMEM),
        compiler_params=pltpu.CompilerParams(vmem_limit_bytes=48 * 2**20),
        name="weight_grad",
    )(x, other, dv)


def attention_kernel(
    len_ref, q_ref, k_ref, v_ref, do_ref, att_ref, dq_ref, dk_ref, dv_ref,
    q_rows, do_rows, bias, probs, dscores,
):
    ctx = lax.axis_index("ctx")
    start = pl.multiple_of(jnp.clip(ctx - 4, 0, 3) * TOK, TOK)
    scale = HEAD_DIM ** -0.5
    for h in range(GROUP):
        q_rows[h * TOK : (h + 1) * TOK] = q_ref[:, h * HEAD_DIM : (h + 1) * HEAD_DIM]
        do_rows[h * TOK : (h + 1) * TOK] = do_ref[:, h * HEAD_DIM : (h + 1) * HEAD_DIM]
    lane = lax.broadcasted_iota(jnp.int32, (1, LANES), 1)
    query = ctx * TOK + lax.rem(lane, TOK)
    first = jnp.zeros_like(query)
    end = jnp.int32(0)
    for d in range(8):
        end = end + len_ref[0, d]
        first = jnp.where(query >= end, end, first)
    key = start + lax.broadcasted_iota(jnp.int32, (WINDOW, LANES), 0)
    bias[...] = jnp.where((key >= first) & (key <= query), F32(0.0), F32(-1e30))

    keys = k_ref[pl.ds(start, WINDOW), :]
    values = v_ref[pl.ds(start, WINDOW), :]
    nt = (((1,), (1,)), ((), ()))
    tn = (((0,), (0,)), ((), ()))
    for i in range(GROUP // HEADS_AT_ONCE):
        cols = slice(i * LANES, (i + 1) * LANES)
        q = q_rows[cols]
        do = do_rows[cols]
        scores = lax.dot_general(keys, q, nt, preferred_element_type=F32)
        scores = scores * F32(scale) + bias[...]
        top = jnp.max(scores, axis=0, keepdims=True)
        weights = jnp.exp(scores - top)
        p = weights * (1.0 / jnp.sum(weights, axis=0, keepdims=True))
        p_half = p.astype(BF16)
        probs[:, cols] = p_half
        att = lax.dot_general(values, p_half, tn, preferred_element_type=F32)
        dp = lax.dot_general(values, do, nt, preferred_element_type=F32)
        dots = jnp.sum(p * dp, axis=0, keepdims=True)
        ds = (p * (dp - dots)).astype(BF16)
        dscores[:, cols] = ds
        dq = lax.dot_general(keys, ds, tn, preferred_element_type=F32) * F32(scale)
        att = att.T.astype(BF16)
        dq = dq.T.astype(BF16)
        for j in range(HEADS_AT_ONCE):
            h = i * HEADS_AT_ONCE + j
            att_ref[:, h * HEAD_DIM : (h + 1) * HEAD_DIM] = att[j * TOK : (j + 1) * TOK]
            dq_ref[:, h * HEAD_DIM : (h + 1) * HEAD_DIM] = dq[j * TOK : (j + 1) * TOK]
    dk_ref[...] = jnp.zeros_like(dk_ref)
    dv_ref[...] = jnp.zeros_like(dv_ref)
    dv_ref[pl.ds(start, WINDOW), :] = jnp.dot(
        probs[...], do_rows[...], preferred_element_type=F32
    ).astype(BF16)
    dk_ref[pl.ds(start, WINDOW), :] = jnp.dot(
        dscores[...], q_rows[...], preferred_element_type=F32
    ).astype(BF16)


def attention(lengths, q, k, v, do):
    vmem = pl.BlockSpec(memory_space=pltpu.VMEM)
    wide = jax.ShapeDtypeStruct((TOK, GROUP * HEAD_DIM), BF16)
    pack = jax.ShapeDtypeStruct((PACK, HEAD_DIM), BF16)
    return pl.pallas_call(
        attention_kernel,
        out_shape=(wide, wide, pack, pack),
        in_specs=[pl.BlockSpec(memory_space=pltpu.SMEM)] + [vmem] * 4,
        out_specs=(vmem,) * 4,
        scratch_shapes=[
            pltpu.VMEM((GROUP * TOK, HEAD_DIM), BF16),
            pltpu.VMEM((GROUP * TOK, HEAD_DIM), BF16),
            pltpu.VMEM((WINDOW, LANES), F32),
            pltpu.VMEM((WINDOW, GROUP * TOK), BF16),
            pltpu.VMEM((WINDOW, GROUP * TOK), BF16),
        ],
        compiler_params=pltpu.CompilerParams(vmem_limit_bytes=56 * 2**20),
        name="attention",
    )(lengths, q, k, v, do)


def summed(parts):
    return jnp.sum(parts.astype(F32), axis=0)


def shards(queries, key_states, normed, value_weight, grad_out, lengths):
    core = lax.axis_index("core")
    quarters = normed.reshape(TOK, 2, 2, 512)
    away = lax.dynamic_index_in_dim(quarters, 1 - core, axis=2, keepdims=False)
    other = lax.ppermute(away.reshape(TOK, 1024), "core", [(0, 1), (1, 0)])

    weight = to_all(swapped_with_mp(value_weight), CHIPS, 64)
    weight = weight.reshape(4, 2, 512, HEAD_DIM)
    parts = project(normed, other, weight)
    projected = summed(
        lax.all_to_all(parts, PAIR_MP, 0, 0, tiled=True)
    ).astype(BF16)
    gathered = to_all(jnp.stack([key_states, projected]), "ctx", 8).reshape(8, 2, TOK, HEAD_DIM)
    keys = gathered[:, 0].reshape(PACK, HEAD_DIM)
    values = gathered[:, 1].reshape(PACK, HEAD_DIM)

    attended, grad_query, dk, dv = attention(lengths, queries, keys, values, grad_out)

    back = jnp.stack([dk.reshape(8, TOK, HEAD_DIM), dv.reshape(8, TOK, HEAD_DIM)], axis=1)
    back = lax.all_to_all(back, "ctx", 0, 0, tiled=True)
    back = summed(back)
    grad_key = (back[0] * F32(HEAD_DIM ** -0.5)).astype(BF16)
    grad_value = back[1].astype(BF16)

    grad_values = to_all(grad_value, PAIR_MP, 8)
    blocks = weight_grad(normed, other, grad_values).reshape(64, 64, HEAD_DIM)
    block = summed(lax.all_to_all(blocks, CHIPS, 0, 0, tiled=True))
    grad_weight = swapped_with_mp(block)
    return attended, grad_query, grad_key, grad_weight


def solution(mesh):
    fine = Mesh(mesh.devices.reshape(2, 4, 2, 8, 4), ("yh", "x", "core", "ctx", "mp"))
    tokens = P(("yh", "x", "core", "ctx"), "mp")
    return jax.shard_map(
        shards,
        mesh=fine,
        in_specs=(tokens,) * 5 + (P(("yh", "x", "core"), None),),
        out_specs=(tokens,) * 4,
        check_vma=False,
    )
```

```python
import jax
import jax.numpy as jnp
from jax import lax
from jax.experimental import pallas as pl
from jax.experimental.pallas import tpu as pltpu
from jax.sharding import Mesh, PartitionSpec as P

HEAD_DIM = 128
TOK = 192
GROUP = 8
REACH = 4
WINDOW = (REACH + 1) * TOK
HEADS_AT_ONCE = 2
LANES = HEADS_AT_ONCE * TOK
CHUNKS = GROUP // HEADS_AT_ONCE
PLANE = ("yh", "x", "mp")
PAIR_MP = ("core", "mp")
SCALE = HEAD_DIM ** -0.5
F32 = jnp.float32
BF16 = jnp.bfloat16
NT = (((1,), (1,)), ((), ()))
TN = (((0,), (0,)), ((), ()))
VMEM = pl.BlockSpec(memory_space=pltpu.VMEM)
SMEM = pl.BlockSpec(memory_space=pltpu.SMEM)


def shape(dims, dtype=BF16):
    return jax.ShapeDtypeStruct(dims, dtype)


def call(kernel, out_shape, n_in, flops, n_bytes, scratch=(), smem=0, vmem=48):
    outs = out_shape if isinstance(out_shape, tuple) else None
    return pl.pallas_call(
        kernel,
        out_shape=out_shape,
        in_specs=[SMEM] * smem + [VMEM] * n_in,
        out_specs=(VMEM,) * len(outs) if outs else VMEM,
        scratch_shapes=scratch,
        compiler_params=pltpu.CompilerParams(vmem_limit_bytes=vmem * 2**20),
        cost_estimate=pl.CostEstimate(
            flops=flops, bytes_accessed=n_bytes, transcendentals=0
        ),
        name=kernel.__name__,
    )


def to_all(block, axes, copies):
    return lax.all_to_all(
        jnp.broadcast_to(block[None], (copies,) + block.shape), axes, 0, 0, tiled=True
    )


def from_behind(block, distance):
    return lax.ppermute(block, "ctx", [(i, i + distance) for i in range(8 - distance)])


def from_ahead(block, distance):
    return lax.ppermute(block, "ctx", [(i + distance, i) for i in range(8 - distance)])


def own_features(x_ref, part):
    core = lax.axis_index("core")
    return x_ref[:, pl.ds(pl.multiple_of((2 * part + core) * 512, 512), 512)]


def other_half(x_ref, out_ref):
    core = lax.axis_index("core")
    for part in range(2):
        place = pl.multiple_of((2 * part + 1 - core) * 512, 512)
        out_ref[:, part * 512 : (part + 1) * 512] = x_ref[:, pl.ds(place, 512)]


def project(x_ref, other_ref, w_ref, *refs):
    dv_refs, out_ref = refs[:-1], refs[-1]
    core = lax.axis_index("core")
    weight = jnp.concatenate(
        [
            jnp.concatenate([w_ref[ctx, part, c] for c in range(4)], axis=1)
            for part in range(2)
            for ctx in range(8)
        ],
        axis=0,
    )
    own = jnp.concatenate([own_features(x_ref, part) for part in range(2)], axis=1)
    for rows, place in ((own, core), (other_ref[...], 1 - core)):
        result = jnp.dot(rows, weight, preferred_element_type=F32)
        for c in range(4):
            out_ref[place * 4 + c, 0] = result[:, c * HEAD_DIM : (c + 1) * HEAD_DIM].astype(BF16)
    total = dv_refs[0][...]
    for ref in dv_refs[1:]:
        total = total + ref[...].astype(F32)
    total = total.astype(BF16)
    for place in range(8):
        out_ref[place, 1] = total


def spread_sum(parts_ref, out_ref):
    total = parts_ref[0, 0].astype(F32)
    for i in range(1, 8):
        total = total + parts_ref[i, 0].astype(F32)
    total = total.astype(BF16)
    for i in range(8):
        out_ref[i] = total


def weight_grad(x_ref, other_ref, dv_ref, out_ref):
    core = lax.axis_index("core")
    own_dv = jnp.concatenate([dv_ref[core * 4 + c, 1] for c in range(4)], axis=1)
    other_dv = jnp.concatenate([dv_ref[(1 - core) * 4 + c, 1] for c in range(4)], axis=1)
    for part in range(2):
        other = other_ref[:, part * 512 : (part + 1) * 512]
        result = lax.dot_general(own_features(x_ref, part), own_dv, TN, preferred_element_type=F32)
        result += lax.dot_general(other, other_dv, TN, preferred_element_type=F32)
        result = result.astype(BF16)
        for ctx in range(8):
            for c in range(4):
                out_ref[ctx, part, c] = result[
                    ctx * 64 : (ctx + 1) * 64, c * HEAD_DIM : (c + 1) * HEAD_DIM
                ]


def tiled_sum(parts_ref, out_ref):
    total = parts_ref[0].astype(F32)
    for i in range(1, 8):
        total = total + parts_ref[i].astype(F32)
    total = total.astype(BF16)
    for i in range(4):
        out_ref[i] = total


def rows_of_heads(wide_ref, rows_ref):
    for h in range(GROUP):
        rows_ref[h * TOK : (h + 1) * TOK] = wide_ref[:, h * HEAD_DIM : (h + 1) * HEAD_DIM]


def fill_bias(len_ref, bias):
    ctx = lax.axis_index("ctx")
    lane = lax.broadcasted_iota(jnp.int32, (1, LANES), 1)
    query = ctx * TOK + lax.rem(lane, TOK)
    first = jnp.zeros_like(query)
    end = jnp.int32(0)
    for d in range(8):
        end = end + len_ref[0, d]
        first = jnp.where(query >= end, end, first)
    offset = lax.broadcasted_iota(jnp.int32, (TOK, LANES), 0)
    for slot in range(REACH + 1):
        key = lax.rem(ctx - (REACH - slot) + 8, 8) * TOK + offset
        bias[slot * TOK : (slot + 1) * TOK] = jnp.where(
            (key >= first) & (key <= query), F32(0.0), F32(-1e30)
        )


def soft(len_ref, q_ref, do_ref, *refs):
    k_refs, dv_refs, stat_ref = refs[:5], refs[5:10], refs[10]
    q_rows, do_rows, bias, probs, keys = refs[11:]
    rows_of_heads(q_ref, q_rows)
    rows_of_heads(do_ref, do_rows)
    for slot, ref in enumerate(k_refs):
        keys[slot * TOK : (slot + 1) * TOK] = ref[...]
    fill_bias(len_ref, bias)
    for i in range(CHUNKS):
        cols = slice(i * LANES, (i + 1) * LANES)
        scores = lax.dot_general(keys[...], q_rows[cols], NT, preferred_element_type=F32)
        scores = scores * F32(SCALE) + bias[...]
        top = jnp.max(scores, axis=0, keepdims=True)
        weights = jnp.exp(scores - top)
        inverse = 1.0 / jnp.sum(weights, axis=0, keepdims=True)
        probs[:, cols] = (weights * inverse).astype(BF16)
        stat_ref[i : i + 1] = top
        stat_ref[CHUNKS + i : CHUNKS + i + 1] = inverse
    total = jnp.dot(probs[...], do_rows[...], preferred_element_type=F32)
    for slot, ref in enumerate(dv_refs):
        ref[...] = total[slot * TOK : (slot + 1) * TOK].astype(ref.dtype)


def attend(len_ref, q_ref, do_ref, stat_ref, v_ref, *refs):
    k_refs, (att_ref, dq_ref), dk_refs = refs[:5], refs[5:7], refs[7:12]
    q_rows, do_rows, bias, dscores, keys, values = refs[12:]
    ctx = lax.axis_index("ctx")
    rows_of_heads(q_ref, q_rows)
    rows_of_heads(do_ref, do_rows)
    for slot, ref in enumerate(k_refs):
        keys[slot * TOK : (slot + 1) * TOK] = ref[...]
        values[slot * TOK : (slot + 1) * TOK] = v_ref[lax.rem(ctx - (REACH - slot) + 8, 8)]
    fill_bias(len_ref, bias)
    for i in range(CHUNKS):
        cols = slice(i * LANES, (i + 1) * LANES)
        scores = lax.dot_general(keys[...], q_rows[cols], NT, preferred_element_type=F32)
        scores = scores * F32(SCALE) + bias[...]
        p = jnp.exp(scores - stat_ref[i : i + 1]) * stat_ref[CHUNKS + i : CHUNKS + i + 1]
        att = lax.dot_general(values[...], p.astype(BF16), TN, preferred_element_type=F32)
        dp = lax.dot_general(values[...], do_rows[cols], NT, preferred_element_type=F32)
        dots = jnp.sum(p * dp, axis=0, keepdims=True)
        ds = (p * (dp - dots)).astype(BF16)
        dscores[:, cols] = ds
        dq = lax.dot_general(keys[...], ds, TN, preferred_element_type=F32) * F32(SCALE)
        att = att.T.astype(BF16)
        dq = dq.T.astype(BF16)
        for j in range(HEADS_AT_ONCE):
            head = slice((i * HEADS_AT_ONCE + j) * HEAD_DIM, (i * HEADS_AT_ONCE + j + 1) * HEAD_DIM)
            att_ref[:, head] = att[j * TOK : (j + 1) * TOK]
            dq_ref[:, head] = dq[j * TOK : (j + 1) * TOK]
    total = jnp.dot(dscores[...], q_rows[...], preferred_element_type=F32)
    for slot, ref in enumerate(dk_refs):
        ref[...] = total[slot * TOK : (slot + 1) * TOK].astype(ref.dtype)


def shards(queries, key_states, normed, value_weight, grad_out, lengths):
    mp = lax.axis_index("mp")
    plane = to_all(value_weight, PLANE, 32)
    mine = lax.dynamic_slice_in_dim(plane, mp * 8, 8, 0)
    spread = jnp.broadcast_to(mine[None], (8, 8, 64, HEAD_DIM))
    away = call(other_half, shape((TOK, 1024)), 1, 0, 10**6)(normed)
    other = lax.ppermute(away, "core", [(0, 1), (1, 0)])
    keys = [from_behind(key_states, d) for d in range(REACH, 0, -1)] + [key_states]
    spread, keys = lax.optimization_barrier((spread, keys))

    weight = lax.all_to_all(spread, "ctx", 0, 0, tiled=True).reshape(8, 2, 4, 64, HEAD_DIM)
    heads = GROUP * TOK
    rows = pltpu.VMEM((heads, HEAD_DIM), BF16)
    window = pltpu.VMEM((WINDOW, HEAD_DIM), BF16)
    bias = pltpu.VMEM((WINDOW, LANES), F32)
    pairs = pltpu.VMEM((WINDOW, heads), BF16)
    block = shape((TOK, HEAD_DIM))
    own = shape((TOK, HEAD_DIM), F32)
    *dv, stats = call(
        soft, (block,) * REACH + (own, shape((8, LANES), F32)), 7, 3 * 10**9, 2 * 10**6,
        (rows, rows, bias, pairs, window), smem=1, vmem=56,
    )(lengths, queries, grad_out, *keys)
    dv = [dv[REACH]] + [from_ahead(dv[REACH - d], d) for d in range(1, REACH + 1)]

    mixed = call(project, shape((8, 2, TOK, HEAD_DIM)), 3 + len(dv), 4 * 10**8, 3 * 10**6)(
        normed, other, weight, *dv
    )
    mixed = lax.all_to_all(mixed, PAIR_MP, 0, 0, tiled=True)
    values = call(spread_sum, shape((8, TOK, HEAD_DIM)), 1, 0, 10**6)(mixed)
    values = lax.all_to_all(values, "ctx", 0, 0, tiled=True)
    partial = call(weight_grad, shape((8, 2, 4, 64, HEAD_DIM)), 3, 4 * 10**8, 3 * 10**6)(
        normed, other, mixed
    )
    partial, values = lax.optimization_barrier((partial, values))
    partial = lax.all_to_all(partial, "ctx", 0, 0, tiled=True)

    wide = shape((TOK, GROUP * HEAD_DIM))
    attended, grad_query, *dk = call(
        attend, (wide, wide) + (block,) * REACH + (own,), 9, 6 * 10**9, 4 * 10**6,
        (rows, rows, bias, pairs, window, window), smem=1, vmem=56,
    )(lengths, queries, grad_out, stats, values, *keys)
    partial, dk = lax.optimization_barrier((partial, dk))
    dk = [dk[REACH]] + [from_ahead(dk[REACH - d], d) for d in range(1, REACH + 1)]
    grad_key = (sum(part.astype(F32) for part in dk) * F32(SCALE)).astype(BF16)

    partial = call(tiled_sum, shape((4, 8, 64, HEAD_DIM)), 1, 0, 2 * 10**6)(
        partial.reshape(8, 8, 64, HEAD_DIM)
    )
    partial = lax.all_to_all(partial.reshape(32, 64, HEAD_DIM), PLANE, 0, 0, tiled=True)
    quarter = lax.axis_index("yh") * 2 + lax.axis_index("x") // 2
    grad_weight = jnp.sum(
        lax.dynamic_index_in_dim(
            partial.reshape(8, 4, 64, HEAD_DIM), quarter, axis=1, keepdims=False
        ).astype(F32),
        axis=0,
    )
    return attended, grad_query, grad_key, grad_weight


def solution(mesh):
    fine = Mesh(mesh.devices.reshape(2, 4, 2, 8, 4), ("yh", "x", "core", "ctx", "mp"))
    tokens = P(("yh", "x", "core", "ctx"), "mp")
    return jax.shard_map(
        shards,
        mesh=fine,
        in_specs=(tokens,) * 5 + (P(("yh", "x", "core"), None),),
        out_specs=(tokens,) * 4,
        check_vma=False,
    )
```

```python
import jax
import jax.numpy as jnp
from jax import lax
from jax.experimental import pallas as pl
from jax.experimental.pallas import tpu as pltpu
from jax.sharding import Mesh, PartitionSpec as P

HEAD_DIM = 128
TOK = 192
GROUP = 8
REACH = 4
WINDOW = (REACH + 1) * TOK
HEADS_AT_ONCE = 2
LANES = HEADS_AT_ONCE * TOK
CHUNKS = GROUP // HEADS_AT_ONCE
CHIPS = ("yh", "x")
SCALE = HEAD_DIM ** -0.5
F32 = jnp.float32
BF16 = jnp.bfloat16
NT = (((1,), (1,)), ((), ()))
TN = (((0,), (0,)), ((), ()))
VMEM = pl.BlockSpec(memory_space=pltpu.VMEM)
SMEM = pl.BlockSpec(memory_space=pltpu.SMEM)


def shape(dims, dtype=BF16):
    return jax.ShapeDtypeStruct(dims, dtype)


def call(kernel, out_shape, n_in, flops, n_bytes, scratch=(), smem=0, vmem=48):
    outs = out_shape if isinstance(out_shape, tuple) else None
    return pl.pallas_call(
        kernel,
        out_shape=out_shape,
        in_specs=[SMEM] * smem + [VMEM] * n_in,
        out_specs=(VMEM,) * len(outs) if outs else VMEM,
        scratch_shapes=scratch,
        compiler_params=pltpu.CompilerParams(vmem_limit_bytes=vmem * 2**20),
        cost_estimate=pl.CostEstimate(
            flops=flops, bytes_accessed=n_bytes, transcendentals=0
        ),
        name=kernel.__name__,
    )


def to_all(block, axes, copies):
    return lax.all_to_all(
        jnp.broadcast_to(block[None], (copies,) + block.shape), axes, 0, 0, tiled=True
    )


def from_behind(block, distance):
    return lax.ppermute(block, "ctx", [(i, i + distance) for i in range(8 - distance)])


def from_ahead(block, distance):
    return lax.ppermute(block, "ctx", [(i + distance, i) for i in range(8 - distance)])


def weight_rows(w_ref, j):
    return jnp.concatenate([w_ref[ctx, j] for ctx in range(8)], axis=0)


def feature_columns(x_ref, j, core):
    place = pl.multiple_of(((j % 2) * 2 + core) * 512, 512)
    return x_ref[j // 2, :, pl.ds(place, 512)]


def project(x_ref, own_ref, other_ref, out_ref):
    core = lax.axis_index("core")
    total = jnp.zeros((TOK, HEAD_DIM), F32)
    for w_ref, half in ((own_ref, core), (other_ref, 1 - core)):
        for j in range(8):
            total += jnp.dot(
                feature_columns(x_ref, j, half), weight_rows(w_ref, j), preferred_element_type=F32
            )
    total = total.astype(BF16)
    for place in range(8):
        out_ref[place] = total


def weight_grad(x_ref, *refs):
    dv_refs, out_refs = refs[:5], refs[5:]
    core = lax.axis_index("core")
    dv = dv_refs[0][...]
    for ref in dv_refs[1:]:
        dv = dv + ref[...].astype(F32)
    dv = dv.astype(BF16)
    for out_ref, half in zip(out_refs, (core, 1 - core)):
        for j in range(8):
            rows = lax.dot_general(
                feature_columns(x_ref, j, half), dv, TN, preferred_element_type=F32
            ).astype(BF16)
            for ctx in range(8):
                out_ref[ctx, j] = rows[ctx * 64 : (ctx + 1) * 64]


def add_halves(a_ref, b_ref, out_ref):
    out_ref[...] = (a_ref[...].astype(F32) + b_ref[...].astype(F32)).astype(BF16)


def sum_blocks(parts_ref, out_ref):
    total = parts_ref[0].astype(F32)
    for i in range(1, 8):
        total = total + parts_ref[i].astype(F32)
    out_ref[...] = total.astype(out_ref.dtype)


def rows_of_heads(wide_ref, rows_ref):
    for h in range(GROUP):
        rows_ref[h * TOK : (h + 1) * TOK] = wide_ref[:, h * HEAD_DIM : (h + 1) * HEAD_DIM]


def fill_bias(len_ref, bias):
    ctx = lax.axis_index("ctx")
    lane = lax.broadcasted_iota(jnp.int32, (1, LANES), 1)
    query = ctx * TOK + lax.rem(lane, TOK)
    first = jnp.zeros_like(query)
    end = jnp.int32(0)
    for d in range(8):
        end = end + len_ref[0, d]
        first = jnp.where(query >= end, end, first)
    offset = lax.broadcasted_iota(jnp.int32, (TOK, LANES), 0)
    for slot in range(REACH + 1):
        key = lax.rem(ctx - (REACH - slot) + 8, 8) * TOK + offset
        bias[slot * TOK : (slot + 1) * TOK] = jnp.where(
            (key >= first) & (key <= query), F32(0.0), F32(-1e30)
        )


def soft(len_ref, q_ref, do_ref, *refs):
    k_refs, dv_refs, stat_ref = refs[:5], refs[5:10], refs[10]
    q_rows, do_rows, bias, probs, keys = refs[11:]
    rows_of_heads(q_ref, q_rows)
    rows_of_heads(do_ref, do_rows)
    for slot, ref in enumerate(k_refs):
        keys[slot * TOK : (slot + 1) * TOK] = ref[...]
    fill_bias(len_ref, bias)
    for i in range(CHUNKS):
        cols = slice(i * LANES, (i + 1) * LANES)
        scores = lax.dot_general(keys[...], q_rows[cols], NT, preferred_element_type=F32)
        scores = scores * F32(SCALE) + bias[...]
        top = jnp.max(scores, axis=0, keepdims=True)
        weights = jnp.exp(scores - top)
        inverse = 1.0 / jnp.sum(weights, axis=0, keepdims=True)
        probs[:, cols] = (weights * inverse).astype(BF16)
        stat_ref[i : i + 1] = top
        stat_ref[CHUNKS + i : CHUNKS + i + 1] = inverse
    total = jnp.dot(probs[...], do_rows[...], preferred_element_type=F32)
    for slot, ref in enumerate(dv_refs):
        ref[...] = total[slot * TOK : (slot + 1) * TOK].astype(ref.dtype)


def attend(len_ref, q_ref, do_ref, stat_ref, v_ref, *refs):
    k_refs, (att_ref, dq_ref), dk_refs = refs[:5], refs[5:7], refs[7:12]
    q_rows, do_rows, bias, dscores, keys, values = refs[12:]
    ctx = lax.axis_index("ctx")
    rows_of_heads(q_ref, q_rows)
    rows_of_heads(do_ref, do_rows)
    for slot, ref in enumerate(k_refs):
        keys[slot * TOK : (slot + 1) * TOK] = ref[...]
        values[slot * TOK : (slot + 1) * TOK] = v_ref[lax.rem(ctx - (REACH - slot) + 8, 8)]
    fill_bias(len_ref, bias)
    for i in range(CHUNKS):
        cols = slice(i * LANES, (i + 1) * LANES)
        scores = lax.dot_general(keys[...], q_rows[cols], NT, preferred_element_type=F32)
        scores = scores * F32(SCALE) + bias[...]
        p = jnp.exp(scores - stat_ref[i : i + 1]) * stat_ref[CHUNKS + i : CHUNKS + i + 1]
        att = lax.dot_general(values[...], p.astype(BF16), TN, preferred_element_type=F32)
        dp = lax.dot_general(values[...], do_rows[cols], NT, preferred_element_type=F32)
        dots = jnp.sum(p * dp, axis=0, keepdims=True)
        ds = (p * (dp - dots)).astype(BF16)
        dscores[:, cols] = ds
        dq = lax.dot_general(keys[...], ds, TN, preferred_element_type=F32) * F32(SCALE)
        att = att.T.astype(BF16)
        dq = dq.T.astype(BF16)
        for j in range(HEADS_AT_ONCE):
            head = slice((i * HEADS_AT_ONCE + j) * HEAD_DIM, (i * HEADS_AT_ONCE + j + 1) * HEAD_DIM)
            att_ref[:, head] = att[j * TOK : (j + 1) * TOK]
            dq_ref[:, head] = dq[j * TOK : (j + 1) * TOK]
    total = jnp.dot(dscores[...], q_rows[...], preferred_element_type=F32)
    for slot, ref in enumerate(dk_refs):
        ref[...] = total[slot * TOK : (slot + 1) * TOK].astype(ref.dtype)


def shards(queries, key_states, normed, value_weight, grad_out, lengths):
    features = lax.all_gather(normed, "mp", axis=0)
    keys = [from_behind(key_states, d) for d in range(REACH, 0, -1)] + [key_states]
    chips = to_all(value_weight, CHIPS, 8)
    spread = jnp.broadcast_to(chips[None], (8, 8, 64, HEAD_DIM))
    spread, keys = lax.optimization_barrier((spread, keys))

    weight = lax.all_to_all(spread, "ctx", 0, 0, tiled=True)
    other = lax.ppermute(weight, "core", [(0, 1), (1, 0)])
    heads = GROUP * TOK
    rows = pltpu.VMEM((heads, HEAD_DIM), BF16)
    window = pltpu.VMEM((WINDOW, HEAD_DIM), BF16)
    bias = pltpu.VMEM((WINDOW, LANES), F32)
    pairs = pltpu.VMEM((WINDOW, heads), BF16)
    block = shape((TOK, HEAD_DIM))
    own = shape((TOK, HEAD_DIM), F32)
    whole = shape((8, 8, 64, HEAD_DIM))
    *dv, stats = call(
        soft, (block,) * REACH + (own, shape((8, LANES), F32)), 7, 3 * 10**9, 2 * 10**6,
        (rows, rows, bias, pairs, window), smem=1, vmem=56,
    )(lengths, queries, grad_out, *keys)
    dv = [dv[REACH]] + [from_ahead(dv[REACH - d], d) for d in range(1, REACH + 1)]

    values = call(project, shape((8, TOK, HEAD_DIM)), 3, 4 * 10**8, 5 * 10**6)(
        features, weight, other
    )
    values = lax.all_to_all(values, "ctx", 0, 0, tiled=True)
    partial, given = call(weight_grad, (whole, whole), 6, 4 * 10**8, 5 * 10**6)(features, *dv)
    taken = lax.ppermute(given, "core", [(0, 1), (1, 0)])
    partial = call(add_halves, whole, 2, 10**6, 3 * 10**6)(partial, taken)
    partial, values = lax.optimization_barrier((partial, values))
    partial = lax.all_to_all(partial, "ctx", 0, 0, tiled=True)

    wide = shape((TOK, GROUP * HEAD_DIM))
    attended, grad_query, *dk = call(
        attend, (wide, wide) + (block,) * REACH + (own,), 9, 6 * 10**9, 4 * 10**6,
        (rows, rows, bias, pairs, window, window), smem=1, vmem=56,
    )(lengths, queries, grad_out, stats, values, *keys)
    partial, dk = lax.optimization_barrier((partial, dk))
    dk = [dk[REACH]] + [from_ahead(dk[REACH - d], d) for d in range(1, REACH + 1)]
    grad_key = (sum(part.astype(F32) for part in dk) * F32(SCALE)).astype(BF16)

    partial = call(sum_blocks, shape((8, 64, HEAD_DIM)), 1, 10**6, 10**6)(partial)
    partial = lax.all_to_all(partial, CHIPS, 0, 0, tiled=True)
    grad_weight = call(sum_blocks, shape((64, HEAD_DIM), F32), 1, 10**5, 10**5)(partial)
    return attended, grad_query, grad_key, grad_weight


def solution(mesh):
    fine = Mesh(mesh.devices.reshape(2, 4, 2, 8, 4), ("yh", "x", "core", "ctx", "mp"))
    tokens = P(("yh", "x", "core", "ctx"), "mp")
    return jax.shard_map(
        shards,
        mesh=fine,
        in_specs=(tokens,) * 5 + (P(("yh", "x", "core"), None),),
        out_specs=(tokens,) * 4,
        check_vma=False,
    )
```

```python
import jax
import jax.numpy as jnp
from jax import lax
from jax.experimental import pallas as pl
from jax.experimental.pallas import tpu as pltpu
from jax.sharding import Mesh, PartitionSpec as P

HEAD_DIM = 128
TOK = 192
GROUP = 8
REACH = 4
WINDOW = (REACH + 1) * TOK
HEADS_AT_ONCE = 2
LANES = HEADS_AT_ONCE * TOK
CHUNKS = GROUP // HEADS_AT_ONCE
PLANE = ("yh", "x1", "mp")
SCALE = HEAD_DIM ** -0.5
F32 = jnp.float32
BF16 = jnp.bfloat16
NT = (((1,), (1,)), ((), ()))
TN = (((0,), (0,)), ((), ()))
VMEM = pl.BlockSpec(memory_space=pltpu.VMEM)
SMEM = pl.BlockSpec(memory_space=pltpu.SMEM)


def shape(dims, dtype=BF16):
    return jax.ShapeDtypeStruct(dims, dtype)


def call(kernel, out_shape, n_in, flops, n_bytes, scratch=(), smem=0, vmem=48):
    outs = out_shape if isinstance(out_shape, tuple) else None
    return pl.pallas_call(
        kernel,
        out_shape=out_shape,
        in_specs=[SMEM] * smem + [VMEM] * n_in,
        out_specs=(VMEM,) * len(outs) if outs else VMEM,
        scratch_shapes=scratch,
        compiler_params=pltpu.CompilerParams(vmem_limit_bytes=vmem * 2**20),
        cost_estimate=pl.CostEstimate(
            flops=flops, bytes_accessed=n_bytes, transcendentals=0
        ),
        name=kernel.__name__,
    )


def to_all(block, axes, copies):
    return lax.all_to_all(
        jnp.broadcast_to(block[None], (copies,) + block.shape), axes, 0, 0, tiled=True
    )


def from_behind(block, distance):
    return lax.ppermute(block, "ctx", [(i, i + distance) for i in range(8 - distance)])


def from_ahead(block, distance):
    return lax.ppermute(block, "ctx", [(i + distance, i) for i in range(8 - distance)])


def traded(blocks):
    both = [(0, 3), (1, 2), (2, 1), (3, 0)]
    pair = [(0, 1), (1, 0)]
    return [
        lax.ppermute(blocks[0], "core", pair),
        lax.ppermute(blocks[1], "x0", pair),
        lax.ppermute(blocks[2], ("x0", "core"), both),
    ]


def piece(x_ref, step):
    x0, core = lax.axis_index("x0"), lax.axis_index("core")
    x0 = 1 - x0 if step >= 2 else x0
    core = 1 - core if step % 2 else core
    return x_ref[:, pl.ds(pl.multiple_of((2 * x0 + core) * 512, 512), 512)]


def pieces(x_ref, *out_refs):
    for step, ref in enumerate(out_refs):
        ref[...] = piece(x_ref, step + 1)


def project(x_ref, *refs):
    others, w_ref, outs = refs[:3], refs[3], refs[4:]
    weight = jnp.concatenate(
        [jnp.concatenate([w_ref[ctx, c] for c in range(4)], axis=1) for ctx in range(8)], axis=0
    )
    rows = [piece(x_ref, 0)] + [ref[...] for ref in others]
    for x, out_ref in zip(rows, outs):
        result = jnp.dot(x, weight, preferred_element_type=F32)
        for c in range(4):
            out_ref[c] = result[:, c * HEAD_DIM : (c + 1) * HEAD_DIM].astype(out_ref.dtype)


def mix(*refs):
    parts, dv_refs, out_ref = refs[:4], refs[4:9], refs[9]
    total = dv_refs[0][...]
    for ref in dv_refs[1:]:
        total = total + ref[...].astype(F32)
    total = total.astype(BF16)
    for c in range(4):
        value = parts[0][c]
        for ref in parts[1:]:
            value = value + ref[c].astype(F32)
        out_ref[c, 0] = value.astype(BF16)
        out_ref[c, 1] = total


def spread_sum(parts_ref, values_ref, dv_ref):
    total = parts_ref[0, 0].astype(F32)
    for i in range(1, 4):
        total = total + parts_ref[i, 0].astype(F32)
    total = total.astype(BF16)
    for i in range(8):
        values_ref[i] = total
    for i in range(4):
        dv_ref[i] = parts_ref[i, 1]


def weight_grad(x_ref, *refs):
    others, dv_refs, out_ref = refs[:3], refs[3:7], refs[7]
    rows = [piece(x_ref, 0)] + [ref[...] for ref in others]
    result = jnp.zeros((512, 512), F32)
    for x, dv_ref in zip(rows, dv_refs):
        dv = jnp.concatenate([dv_ref[c] for c in range(4)], axis=1)
        result += lax.dot_general(x, dv, TN, preferred_element_type=F32)
    result = result.astype(BF16)
    for ctx in range(8):
        for c in range(4):
            out_ref[ctx, c] = result[ctx * 64 : (ctx + 1) * 64, c * HEAD_DIM : (c + 1) * HEAD_DIM]


def tiled_sum(parts_ref, out_ref):
    total = parts_ref[0].astype(F32)
    for i in range(1, 8):
        total = total + parts_ref[i].astype(F32)
    total = total.astype(BF16)
    for i in range(4):
        out_ref[i] = total


def rows_of_heads(wide_ref, rows_ref):
    for h in range(GROUP):
        rows_ref[h * TOK : (h + 1) * TOK] = wide_ref[:, h * HEAD_DIM : (h + 1) * HEAD_DIM]


def fill_bias(len_ref, bias):
    ctx = lax.axis_index("ctx")
    lane = lax.broadcasted_iota(jnp.int32, (1, LANES), 1)
    query = ctx * TOK + lax.rem(lane, TOK)
    first = jnp.zeros_like(query)
    end = jnp.int32(0)
    for d in range(8):
        end = end + len_ref[0, d]
        first = jnp.where(query >= end, end, first)
    offset = lax.broadcasted_iota(jnp.int32, (TOK, LANES), 0)
    for slot in range(REACH + 1):
        key = lax.rem(ctx - (REACH - slot) + 8, 8) * TOK + offset
        bias[slot * TOK : (slot + 1) * TOK] = jnp.where(
            (key >= first) & (key <= query), F32(0.0), F32(-1e30)
        )


def soft(len_ref, q_ref, do_ref, *refs):
    k_refs, dv_refs, stat_ref = refs[:5], refs[5:10], refs[10]
    q_rows, do_rows, bias, probs, keys = refs[11:]
    rows_of_heads(q_ref, q_rows)
    rows_of_heads(do_ref, do_rows)
    for slot, ref in enumerate(k_refs):
        keys[slot * TOK : (slot + 1) * TOK] = ref[...]
    fill_bias(len_ref, bias)
    for i in range(CHUNKS):
        cols = slice(i * LANES, (i + 1) * LANES)
        scores = lax.dot_general(keys[...], q_rows[cols], NT, preferred_element_type=F32)
        scores = scores * F32(SCALE) + bias[...]
        top = jnp.max(scores, axis=0, keepdims=True)
        weights = jnp.exp(scores - top)
        inverse = 1.0 / jnp.sum(weights, axis=0, keepdims=True)
        probs[:, cols] = (weights * inverse).astype(BF16)
        stat_ref[i : i + 1] = top
        stat_ref[CHUNKS + i : CHUNKS + i + 1] = inverse
    total = jnp.dot(probs[...], do_rows[...], preferred_element_type=F32)
    for slot, ref in enumerate(dv_refs):
        ref[...] = total[slot * TOK : (slot + 1) * TOK].astype(ref.dtype)


def attend(len_ref, q_ref, do_ref, stat_ref, v_ref, *refs):
    k_refs, (att_ref, dq_ref), dk_refs = refs[:5], refs[5:7], refs[7:12]
    q_rows, do_rows, bias, dscores, keys, values = refs[12:]
    ctx = lax.axis_index("ctx")
    rows_of_heads(q_ref, q_rows)
    rows_of_heads(do_ref, do_rows)
    for slot, ref in enumerate(k_refs):
        keys[slot * TOK : (slot + 1) * TOK] = ref[...]
        values[slot * TOK : (slot + 1) * TOK] = v_ref[lax.rem(ctx - (REACH - slot) + 8, 8)]
    fill_bias(len_ref, bias)
    for i in range(CHUNKS):
        cols = slice(i * LANES, (i + 1) * LANES)
        scores = lax.dot_general(keys[...], q_rows[cols], NT, preferred_element_type=F32)
        scores = scores * F32(SCALE) + bias[...]
        p = jnp.exp(scores - stat_ref[i : i + 1]) * stat_ref[CHUNKS + i : CHUNKS + i + 1]
        att = lax.dot_general(values[...], p.astype(BF16), TN, preferred_element_type=F32)
        dp = lax.dot_general(values[...], do_rows[cols], NT, preferred_element_type=F32)
        dots = jnp.sum(p * dp, axis=0, keepdims=True)
        ds = (p * (dp - dots)).astype(BF16)
        dscores[:, cols] = ds
        dq = lax.dot_general(keys[...], ds, TN, preferred_element_type=F32) * F32(SCALE)
        att = att.T.astype(BF16)
        dq = dq.T.astype(BF16)
        for j in range(HEADS_AT_ONCE):
            head = slice((i * HEADS_AT_ONCE + j) * HEAD_DIM, (i * HEADS_AT_ONCE + j + 1) * HEAD_DIM)
            att_ref[:, head] = att[j * TOK : (j + 1) * TOK]
            dq_ref[:, head] = dq[j * TOK : (j + 1) * TOK]
    total = jnp.dot(dscores[...], q_rows[...], preferred_element_type=F32)
    for slot, ref in enumerate(dk_refs):
        ref[...] = total[slot * TOK : (slot + 1) * TOK].astype(ref.dtype)


def shards(queries, key_states, normed, value_weight, grad_out, lengths):
    mp = lax.axis_index("mp")
    plane = to_all(value_weight, PLANE, 16)
    mine = lax.dynamic_slice_in_dim(plane, mp * 4, 4, 0)
    spread = jnp.broadcast_to(mine[None], (8, 4, 64, HEAD_DIM))
    quarter = shape((TOK, 512))
    others = traded(call(pieces, (quarter,) * 3, 1, 0, 10**6)(normed))
    keys = [from_behind(key_states, d) for d in range(REACH, 0, -1)] + [key_states]
    spread, keys = lax.optimization_barrier((spread, keys))

    weight = lax.all_to_all(spread, "ctx", 0, 0, tiled=True)
    heads = GROUP * TOK
    rows = pltpu.VMEM((heads, HEAD_DIM), BF16)
    window = pltpu.VMEM((WINDOW, HEAD_DIM), BF16)
    bias = pltpu.VMEM((WINDOW, LANES), F32)
    pairs = pltpu.VMEM((WINDOW, heads), BF16)
    block = shape((TOK, HEAD_DIM))
    own = shape((TOK, HEAD_DIM), F32)
    *dv, stats = call(
        soft, (block,) * REACH + (own, shape((8, LANES), F32)), 7, 3 * 10**9, 2 * 10**6,
        (rows, rows, bias, pairs, window), smem=1, vmem=56,
    )(lengths, queries, grad_out, *keys)
    dv = [dv[REACH]] + [from_ahead(dv[REACH - d], d) for d in range(1, REACH + 1)]
    weight, stats = lax.optimization_barrier((weight, stats))

    four = shape((4, TOK, HEAD_DIM))
    projected, *away = call(
        project, (shape((4, TOK, HEAD_DIM), F32),) + (four,) * 3, 5, 4 * 10**8, 3 * 10**6
    )(normed, *others, weight)
    mixed = call(mix, shape((4, 2, TOK, HEAD_DIM)), 9, 10**6, 2 * 10**6)(
        projected, *traded(away), *dv
    )
    mixed = lax.all_to_all(mixed, "mp", 0, 0, tiled=True)
    values, grad_value = call(spread_sum, (shape((8, TOK, HEAD_DIM)), four), 1, 10**6, 10**6)(mixed)
    values = lax.all_to_all(values, "ctx", 0, 0, tiled=True)
    partial = call(weight_grad, shape((8, 4, 64, HEAD_DIM)), 8, 4 * 10**8, 3 * 10**6)(
        normed, *others, grad_value, *traded([grad_value] * 3)
    )
    partial, values = lax.optimization_barrier((partial, values))
    partial = lax.all_to_all(partial, "ctx", 0, 0, tiled=True)

    wide = shape((TOK, GROUP * HEAD_DIM))
    attended, grad_query, *dk = call(
        attend, (wide, wide) + (block,) * REACH + (own,), 9, 6 * 10**9, 4 * 10**6,
        (rows, rows, bias, pairs, window, window), smem=1, vmem=56,
    )(lengths, queries, grad_out, stats, values, *keys)
    partial, dk = lax.optimization_barrier((partial, dk))
    dk = [dk[REACH]] + [from_ahead(dk[REACH - d], d) for d in range(1, REACH + 1)]
    grad_key = (sum(part.astype(F32) for part in dk) * F32(SCALE)).astype(BF16)

    partial = call(tiled_sum, shape((4, 4, 64, HEAD_DIM)), 1, 10**6, 10**6)(partial)
    partial = lax.all_to_all(partial.reshape(16, 64, HEAD_DIM), PLANE, 0, 0, tiled=True)
    place = lax.axis_index("yh") * 2 + lax.axis_index("x1")
    grad_weight = jnp.sum(
        lax.dynamic_index_in_dim(
            partial.reshape(4, 4, 64, HEAD_DIM), place, axis=1, keepdims=False
        ).astype(F32),
        axis=0,
    )
    return attended, grad_query, grad_key, grad_weight


def solution(mesh):
    axes = ("yh", "x1", "x0", "core", "ctx", "mp")
    fine = Mesh(mesh.devices.reshape(2, 2, 2, 2, 8, 4), axes)
    tokens = P(axes[:5], "mp")
    return jax.shard_map(
        shards,
        mesh=fine,
        in_specs=(tokens,) * 5 + (P(axes[:4], None),),
        out_specs=(tokens,) * 4,
        check_vma=False,
    )
```

```python
import jax
import jax.numpy as jnp
from jax import lax
from jax.experimental import pallas as pl
from jax.experimental.pallas import tpu as pltpu
from jax.sharding import Mesh, PartitionSpec as P

HEAD_DIM = 128
TOK = 192
GROUP = 8
REACH = 4
WINDOW = (REACH + 1) * TOK
HEADS_AT_ONCE = 2
LANES = HEADS_AT_ONCE * TOK
CHUNKS = GROUP // HEADS_AT_ONCE
PLANE = ("yh", "x1", "ctx")
SCALE = HEAD_DIM ** -0.5
F32 = jnp.float32
BF16 = jnp.bfloat16
NT = (((1,), (1,)), ((), ()))
TN = (((0,), (0,)), ((), ()))
VMEM = pl.BlockSpec(memory_space=pltpu.VMEM)
SMEM = pl.BlockSpec(memory_space=pltpu.SMEM)


def shape(dims, dtype=BF16):
    return jax.ShapeDtypeStruct(dims, dtype)


def call(kernel, out_shape, n_in, flops, n_bytes, scratch=(), smem=0, vmem=48):
    outs = out_shape if isinstance(out_shape, tuple) else None
    return pl.pallas_call(
        kernel,
        out_shape=out_shape,
        in_specs=[SMEM] * smem + [VMEM] * n_in,
        out_specs=(VMEM,) * len(outs) if outs else VMEM,
        scratch_shapes=scratch,
        compiler_params=pltpu.CompilerParams(vmem_limit_bytes=vmem * 2**20),
        cost_estimate=pl.CostEstimate(
            flops=flops, bytes_accessed=n_bytes, transcendentals=0
        ),
        name=kernel.__name__,
    )


def to_all(block, axes, copies):
    return lax.all_to_all(
        jnp.broadcast_to(block[None], (copies,) + block.shape), axes, 0, 0, tiled=True
    )


def from_behind(block, distance):
    return lax.ppermute(block, "ctx", [(i, i + distance) for i in range(8 - distance)])


def swapped_with_mp(block):
    route = [(q * 4 + mp, mp * 4 + q) for q in range(4) for mp in range(4)]
    return lax.ppermute(block, ("yh", "x1", "mp"), route)


def summed_over_ctx(parts):
    return lax.psum_scatter(
        parts.reshape(8 * TOK, HEAD_DIM), "ctx", scatter_dimension=0, tiled=True
    )


def traded(blocks):
    both = [(0, 3), (1, 2), (2, 1), (3, 0)]
    pair = [(0, 1), (1, 0)]
    return [
        lax.ppermute(blocks[0], "core", pair),
        lax.ppermute(blocks[1], "x0", pair),
        lax.ppermute(blocks[2], ("x0", "core"), both),
    ]


def piece(x_ref, step):
    x0, core = lax.axis_index("x0"), lax.axis_index("core")
    x0 = 1 - x0 if step >= 2 else x0
    core = 1 - core if step % 2 else core
    return x_ref[:, pl.ds(pl.multiple_of((2 * x0 + core) * 512, 512), 512)]


def pieces(x_ref, *out_refs):
    for step, ref in enumerate(out_refs):
        ref[...] = piece(x_ref, step + 1)


def project(x_ref, *refs):
    others, w_ref, outs = refs[:3], refs[3], refs[4:]
    weight = jnp.concatenate(
        [jnp.concatenate([w_ref[c, ctx] for c in range(4)], axis=1) for ctx in range(8)], axis=0
    )
    rows = [piece(x_ref, 0)] + [ref[...] for ref in others]
    for x, out_ref in zip(rows, outs):
        result = jnp.dot(x, weight, preferred_element_type=F32)
        for c in range(4):
            out_ref[c] = result[:, c * HEAD_DIM : (c + 1) * HEAD_DIM].astype(out_ref.dtype)


def mix(*refs):
    parts, out_ref = refs[:4], refs[4]
    for c in range(4):
        value = parts[0][c]
        for ref in parts[1:]:
            value = value + ref[c].astype(F32)
        out_ref[c] = value.astype(BF16)


def sum_of(parts_ref):
    total = parts_ref[0].astype(F32)
    for i in range(1, parts_ref.shape[0]):
        total = total + parts_ref[i].astype(F32)
    return total


def spread_sum(parts_ref, out_ref):
    total = sum_of(parts_ref).astype(BF16)
    for i in range(8):
        out_ref[i] = total


def sum_blocks(parts_ref, out_ref):
    out_ref[...] = sum_of(parts_ref)


def weight_grad(x_ref, *refs):
    others, dv_refs, out_ref = refs[:3], refs[3:7], refs[7]
    rows = [piece(x_ref, 0)] + [ref[...] for ref in others]
    result = jnp.zeros((512, 512), F32)
    for x, dv_ref in zip(rows, dv_refs):
        dv = jnp.concatenate([dv_ref[c] for c in range(4)], axis=1)
        result += lax.dot_general(x, dv, TN, preferred_element_type=F32)
    result = result.astype(BF16)
    for ctx in range(8):
        for c in range(4):
            out_ref[c, ctx] = result[ctx * 64 : (ctx + 1) * 64, c * HEAD_DIM : (c + 1) * HEAD_DIM]


def rows_of_heads(wide_ref, rows_ref):
    for h in range(GROUP):
        rows_ref[h * TOK : (h + 1) * TOK] = wide_ref[:, h * HEAD_DIM : (h + 1) * HEAD_DIM]


def slot_owner(slot):
    return lax.rem(lax.axis_index("ctx") - (REACH - slot) + 8, 8)


def place_slots(total, out_ref):
    out_ref[...] = jnp.zeros_like(out_ref)
    for slot in range(REACH + 1):
        out_ref[slot_owner(slot)] = total[slot * TOK : (slot + 1) * TOK]


def fill_bias(len_ref, bias):
    ctx = lax.axis_index("ctx")
    lane = lax.broadcasted_iota(jnp.int32, (1, LANES), 1)
    query = ctx * TOK + lax.rem(lane, TOK)
    first = jnp.zeros_like(query)
    end = jnp.int32(0)
    for d in range(8):
        end = end + len_ref[0, d]
        first = jnp.where(query >= end, end, first)
    offset = lax.broadcasted_iota(jnp.int32, (TOK, LANES), 0)
    for slot in range(REACH + 1):
        key = slot_owner(slot) * TOK + offset
        bias[slot * TOK : (slot + 1) * TOK] = jnp.where(
            (key >= first) & (key <= query), F32(0.0), F32(-1e30)
        )


def soft(len_ref, q_ref, do_ref, *refs):
    k_refs, dv_ref, stat_ref = refs[:5], refs[5], refs[6]
    q_rows, do_rows, bias, probs, keys = refs[7:]
    rows_of_heads(q_ref, q_rows)
    rows_of_heads(do_ref, do_rows)
    for slot, ref in enumerate(k_refs):
        keys[slot * TOK : (slot + 1) * TOK] = ref[...]
    fill_bias(len_ref, bias)
    for i in range(CHUNKS):
        cols = slice(i * LANES, (i + 1) * LANES)
        scores = lax.dot_general(keys[...], q_rows[cols], NT, preferred_element_type=F32)
        scores = scores * F32(SCALE) + bias[...]
        top = jnp.max(scores, axis=0, keepdims=True)
        weights = jnp.exp(scores - top)
        inverse = 1.0 / jnp.sum(weights, axis=0, keepdims=True)
        probs[:, cols] = (weights * inverse).astype(BF16)
        stat_ref[i : i + 1] = top
        stat_ref[CHUNKS + i : CHUNKS + i + 1] = inverse
    place_slots(jnp.dot(probs[...], do_rows[...], preferred_element_type=F32), dv_ref)


def attend(len_ref, q_ref, do_ref, stat_ref, v_ref, *refs):
    k_refs, (att_ref, dq_ref, dk_ref) = refs[:5], refs[5:8]
    q_rows, do_rows, bias, dscores, keys, values = refs[8:]
    rows_of_heads(q_ref, q_rows)
    rows_of_heads(do_ref, do_rows)
    for slot, ref in enumerate(k_refs):
        keys[slot * TOK : (slot + 1) * TOK] = ref[...]
        values[slot * TOK : (slot + 1) * TOK] = v_ref[slot_owner(slot)]
    fill_bias(len_ref, bias)
    for i in range(CHUNKS):
        cols = slice(i * LANES, (i + 1) * LANES)
        scores = lax.dot_general(keys[...], q_rows[cols], NT, preferred_element_type=F32)
        scores = scores * F32(SCALE) + bias[...]
        p = jnp.exp(scores - stat_ref[i : i + 1]) * stat_ref[CHUNKS + i : CHUNKS + i + 1]
        att = lax.dot_general(values[...], p.astype(BF16), TN, preferred_element_type=F32)
        dp = lax.dot_general(values[...], do_rows[cols], NT, preferred_element_type=F32)
        dots = jnp.sum(p * dp, axis=0, keepdims=True)
        ds = (p * (dp - dots)).astype(BF16)
        dscores[:, cols] = ds
        dq = lax.dot_general(keys[...], ds, TN, preferred_element_type=F32) * F32(SCALE)
        att = att.T.astype(BF16)
        dq = dq.T.astype(BF16)
        for j in range(HEADS_AT_ONCE):
            head = slice((i * HEADS_AT_ONCE + j) * HEAD_DIM, (i * HEADS_AT_ONCE + j + 1) * HEAD_DIM)
            att_ref[:, head] = att[j * TOK : (j + 1) * TOK]
            dq_ref[:, head] = dq[j * TOK : (j + 1) * TOK]
    place_slots(jnp.dot(dscores[...], q_rows[...], preferred_element_type=F32), dk_ref)


def shards(queries, key_states, normed, value_weight, grad_out, lengths):
    turned = swapped_with_mp(value_weight)
    keys = [from_behind(key_states, d) for d in range(REACH, 0, -1)] + [key_states]
    weight = to_all(turned, PLANE, 32).reshape(4, 8, 64, HEAD_DIM)
    quarter = shape((TOK, 512))
    others = traded(call(pieces, (quarter,) * 3, 1, 0, 10**6)(normed))
    others, lengths = lax.optimization_barrier((others, lengths))

    heads = GROUP * TOK
    rows = pltpu.VMEM((heads, HEAD_DIM), BF16)
    window = pltpu.VMEM((WINDOW, HEAD_DIM), BF16)
    bias = pltpu.VMEM((WINDOW, LANES), F32)
    pairs = pltpu.VMEM((WINDOW, heads), BF16)
    slots = shape((8, TOK, HEAD_DIM), F32)
    dv, stats = call(
        soft, (slots, shape((8, LANES), F32)), 7, 3 * 10**9, 2 * 10**6,
        (rows, rows, bias, pairs, window), smem=1, vmem=56,
    )(lengths, queries, grad_out, *keys)
    weight, stats = lax.optimization_barrier((weight, stats))
    dv = summed_over_ctx(dv)

    four = shape((4, TOK, HEAD_DIM))
    projected, *away = call(
        project, (shape((4, TOK, HEAD_DIM), F32),) + (four,) * 3, 5, 4 * 10**8, 3 * 10**6
    )(normed, *others, weight)
    mixed = call(mix, four, 4, 10**6, 2 * 10**6)(projected, *traded(away))
    mixed = lax.all_to_all(mixed, "mp", 0, 0, tiled=True)
    values = call(spread_sum, shape((8, TOK, HEAD_DIM)), 1, 10**6, 10**6)(mixed)
    values = lax.all_to_all(values, "ctx", 0, 0, tiled=True)

    dv, values = lax.optimization_barrier((dv, values))
    grad_value = to_all(dv.astype(BF16), "mp", 4)
    wide = shape((TOK, GROUP * HEAD_DIM))
    attended, grad_query, dk = call(
        attend, (wide, wide, slots), 9, 6 * 10**9, 4 * 10**6,
        (rows, rows, bias, pairs, window, window), smem=1, vmem=56,
    )(lengths, queries, grad_out, stats, values, *keys)
    grad_key = (summed_over_ctx(dk) * F32(SCALE)).astype(BF16)

    partial = call(weight_grad, shape((4, 8, 64, HEAD_DIM)), 8, 4 * 10**8, 3 * 10**6)(
        normed, *others, grad_value, *traded([grad_value] * 3)
    )
    partial = lax.all_to_all(partial.reshape(32, 64, HEAD_DIM), PLANE, 0, 0, tiled=True)
    total = call(sum_blocks, shape((64, HEAD_DIM), F32), 1, 10**6, 10**6)(partial)
    return attended, grad_query, grad_key, swapped_with_mp(total)


def solution(mesh):
    axes = ("yh", "x1", "x0", "core", "ctx", "mp")
    fine = Mesh(mesh.devices.reshape(2, 2, 2, 2, 8, 4), axes)
    tokens = P(axes[:5], "mp")
    return jax.shard_map(
        shards,
        mesh=fine,
        in_specs=(tokens,) * 5 + (P(axes[:4], None),),
        out_specs=(tokens,) * 4,
        check_vma=False,
    )
```

```python
import jax
import jax.numpy as jnp
from jax import lax
from jax.experimental import pallas as pl
from jax.experimental.pallas import tpu as pltpu
from jax.sharding import Mesh, PartitionSpec as P

HEAD_DIM = 128
TOK = 192
GROUP = 8
REACH = 4
WINDOW = (REACH + 1) * TOK
HEADS_AT_ONCE = 2
LANES = HEADS_AT_ONCE * TOK
CHUNKS = GROUP // HEADS_AT_ONCE
CHIPS = ("yh", "x")
SCALE = HEAD_DIM ** -0.5
F32 = jnp.float32
BF16 = jnp.bfloat16
NT = (((1,), (1,)), ((), ()))
TN = (((0,), (0,)), ((), ()))
VMEM = pl.BlockSpec(memory_space=pltpu.VMEM)
SMEM = pl.BlockSpec(memory_space=pltpu.SMEM)


def shape(dims, dtype=BF16):
    return jax.ShapeDtypeStruct(dims, dtype)


def call(kernel, out_shape, n_in, flops, n_bytes, scratch=(), smem=0, vmem=48):
    outs = out_shape if isinstance(out_shape, tuple) else None
    return pl.pallas_call(
        kernel,
        out_shape=out_shape,
        in_specs=[SMEM] * smem + [VMEM] * n_in,
        out_specs=(VMEM,) * len(outs) if outs else VMEM,
        scratch_shapes=scratch,
        compiler_params=pltpu.CompilerParams(vmem_limit_bytes=vmem * 2**20),
        cost_estimate=pl.CostEstimate(
            flops=flops, bytes_accessed=n_bytes, transcendentals=0
        ),
        name=kernel.__name__,
    )


def to_all(block, axes, copies):
    return lax.all_to_all(
        jnp.broadcast_to(block[None], (copies,) + block.shape), axes, 0, 0, tiled=True
    )


def from_behind(block, distance):
    return lax.ppermute(block, "ctx", [(i, i + distance) for i in range(8 - distance)])


def from_ahead(block, distance):
    return lax.ppermute(block, "ctx", [(i + distance, i) for i in range(8 - distance)])


def weight_rows(w_ref, j):
    return jnp.concatenate([w_ref[ctx, j] for ctx in range(8)], axis=0)


def feature_columns(x_ref, j, core):
    place = pl.multiple_of(((j % 2) * 2 + core) * 512, 512)
    return x_ref[j // 2, :, pl.ds(place, 512)]


def project(x_ref, own_ref, other_ref, out_ref):
    core = lax.axis_index("core")
    total = jnp.zeros((TOK, HEAD_DIM), F32)
    for w_ref, half in ((own_ref, core), (other_ref, 1 - core)):
        for j in range(8):
            total += jnp.dot(
                feature_columns(x_ref, j, half), weight_rows(w_ref, j), preferred_element_type=F32
            )
    out_ref[...] = total.astype(BF16)


def weight_grad(x_ref, *refs):
    dv_refs, out_refs = refs[:5], refs[5:]
    core = lax.axis_index("core")
    dv = dv_refs[0][...]
    for ref in dv_refs[1:]:
        dv = dv + ref[...].astype(F32)
    dv = dv.astype(BF16)
    for out_ref, half in zip(out_refs, (core, 1 - core)):
        for j in range(8):
            rows = lax.dot_general(
                feature_columns(x_ref, j, half), dv, TN, preferred_element_type=F32
            ).astype(BF16)
            for ctx in range(8):
                out_ref[j, ctx] = rows[ctx * 64 : (ctx + 1) * 64]


def add_halves(a_ref, b_ref, out_ref):
    out_ref[...] = (a_ref[...].astype(F32) + b_ref[...].astype(F32)).astype(BF16)


def sum_blocks(parts_ref, out_ref):
    total = parts_ref[0].astype(F32)
    for i in range(1, parts_ref.shape[0]):
        total = total + parts_ref[i].astype(F32)
    out_ref[...] = total


def rows_of_heads(wide_ref, rows_ref):
    for h in range(GROUP):
        rows_ref[h * TOK : (h + 1) * TOK] = wide_ref[:, h * HEAD_DIM : (h + 1) * HEAD_DIM]


def fill_bias(len_ref, bias):
    ctx = lax.axis_index("ctx")
    lane = lax.broadcasted_iota(jnp.int32, (1, LANES), 1)
    query = ctx * TOK + lax.rem(lane, TOK)
    first = jnp.zeros_like(query)
    end = jnp.int32(0)
    for d in range(8):
        end = end + len_ref[0, d]
        first = jnp.where(query >= end, end, first)
    offset = lax.broadcasted_iota(jnp.int32, (TOK, LANES), 0)
    for slot in range(REACH + 1):
        key = lax.rem(ctx - (REACH - slot) + 8, 8) * TOK + offset
        bias[slot * TOK : (slot + 1) * TOK] = jnp.where(
            (key >= first) & (key <= query), F32(0.0), F32(-1e30)
        )


def soft(len_ref, q_ref, do_ref, *refs):
    k_refs, dv_refs, stat_ref = refs[:5], refs[5:10], refs[10]
    q_rows, do_rows, bias, probs, keys = refs[11:]
    rows_of_heads(q_ref, q_rows)
    rows_of_heads(do_ref, do_rows)
    for slot, ref in enumerate(k_refs):
        keys[slot * TOK : (slot + 1) * TOK] = ref[...]
    fill_bias(len_ref, bias)
    for i in range(CHUNKS):
        cols = slice(i * LANES, (i + 1) * LANES)
        scores = lax.dot_general(keys[...], q_rows[cols], NT, preferred_element_type=F32)
        scores = scores * F32(SCALE) + bias[...]
        top = jnp.max(scores, axis=0, keepdims=True)
        weights = jnp.exp(scores - top)
        inverse = 1.0 / jnp.sum(weights, axis=0, keepdims=True)
        probs[:, cols] = (weights * inverse).astype(BF16)
        stat_ref[i : i + 1] = top
        stat_ref[CHUNKS + i : CHUNKS + i + 1] = inverse
    total = jnp.dot(probs[...], do_rows[...], preferred_element_type=F32)
    for slot, ref in enumerate(dv_refs):
        ref[...] = total[slot * TOK : (slot + 1) * TOK].astype(ref.dtype)


def attend(len_ref, q_ref, do_ref, stat_ref, *refs):
    k_refs, v_refs, (att_ref, dq_ref), dk_refs = refs[:5], refs[5:10], refs[10:12], refs[12:17]
    q_rows, do_rows, bias, dscores, keys, values = refs[17:]
    rows_of_heads(q_ref, q_rows)
    rows_of_heads(do_ref, do_rows)
    for slot in range(REACH + 1):
        keys[slot * TOK : (slot + 1) * TOK] = k_refs[slot][...]
        values[slot * TOK : (slot + 1) * TOK] = v_refs[slot][...]
    fill_bias(len_ref, bias)
    for i in range(CHUNKS):
        cols = slice(i * LANES, (i + 1) * LANES)
        scores = lax.dot_general(keys[...], q_rows[cols], NT, preferred_element_type=F32)
        scores = scores * F32(SCALE) + bias[...]
        p = jnp.exp(scores - stat_ref[i : i + 1]) * stat_ref[CHUNKS + i : CHUNKS + i + 1]
        att = lax.dot_general(values[...], p.astype(BF16), TN, preferred_element_type=F32)
        dp = lax.dot_general(values[...], do_rows[cols], NT, preferred_element_type=F32)
        dots = jnp.sum(p * dp, axis=0, keepdims=True)
        ds = (p * (dp - dots)).astype(BF16)
        dscores[:, cols] = ds
        dq = lax.dot_general(keys[...], ds, TN, preferred_element_type=F32) * F32(SCALE)
        att = att.T.astype(BF16)
        dq = dq.T.astype(BF16)
        for j in range(HEADS_AT_ONCE):
            head = slice((i * HEADS_AT_ONCE + j) * HEAD_DIM, (i * HEADS_AT_ONCE + j + 1) * HEAD_DIM)
            att_ref[:, head] = att[j * TOK : (j + 1) * TOK]
            dq_ref[:, head] = dq[j * TOK : (j + 1) * TOK]
    total = jnp.dot(dscores[...], q_rows[...], preferred_element_type=F32)
    for slot, ref in enumerate(dk_refs):
        ref[...] = total[slot * TOK : (slot + 1) * TOK].astype(ref.dtype)


def shards(queries, key_states, normed, value_weight, grad_out, lengths):
    features = lax.all_gather(normed, "mp", axis=0)
    keys = [from_behind(key_states, d) for d in range(REACH, 0, -1)] + [key_states]
    chips = to_all(value_weight, CHIPS, 8)
    spread = jnp.broadcast_to(chips[None], (8, 8, 64, HEAD_DIM))
    spread, keys = lax.optimization_barrier((spread, keys))

    weight = lax.all_to_all(spread, "ctx", 0, 0, tiled=True)
    heads = GROUP * TOK
    rows = pltpu.VMEM((heads, HEAD_DIM), BF16)
    window = pltpu.VMEM((WINDOW, HEAD_DIM), BF16)
    bias = pltpu.VMEM((WINDOW, LANES), F32)
    pairs = pltpu.VMEM((WINDOW, heads), BF16)
    block = shape((TOK, HEAD_DIM))
    own = shape((TOK, HEAD_DIM), F32)
    whole = shape((8, 8, 64, HEAD_DIM))
    *dv, stats = call(
        soft, (block,) * REACH + (own, shape((8, LANES), F32)), 7, 3 * 10**9, 2 * 10**6,
        (rows, rows, bias, pairs, window), smem=1, vmem=56,
    )(lengths, queries, grad_out, *keys)
    dv = [dv[REACH]] + [from_ahead(dv[REACH - d], d) for d in range(1, REACH + 1)]

    weight, dv = lax.optimization_barrier((weight, dv))
    other = lax.ppermute(weight, "core", [(0, 1), (1, 0)])
    other, dv = lax.optimization_barrier((other, dv))

    partial, given = call(weight_grad, (whole, whole), 6, 4 * 10**8, 5 * 10**6)(features, *dv)
    taken = lax.ppermute(given, "core", [(0, 1), (1, 0)])
    projected = call(project, block, 3, 4 * 10**8, 5 * 10**6)(features, weight, other)
    taken, projected = lax.optimization_barrier((taken, projected))
    values = [from_behind(projected, d) for d in range(REACH, 0, -1)] + [projected]
    partial = call(add_halves, whole, 2, 10**6, 3 * 10**6)(partial, taken)
    partial = lax.all_to_all(
        partial.reshape(64, 64, HEAD_DIM), ("yh", "x", "ctx"), 0, 0, tiled=True
    )

    wide = shape((TOK, GROUP * HEAD_DIM))
    attended, grad_query, *dk = call(
        attend, (wide, wide) + (block,) * REACH + (own,), 13, 6 * 10**9, 4 * 10**6,
        (rows, rows, bias, pairs, window, window), smem=1, vmem=56,
    )(lengths, queries, grad_out, stats, *keys, *values)
    dk = [dk[REACH]] + [from_ahead(dk[REACH - d], d) for d in range(1, REACH + 1)]
    grad_key = (sum(part.astype(F32) for part in dk) * F32(SCALE)).astype(BF16)

    partial, grad_key = lax.optimization_barrier((partial, grad_key))
    grad_weight = call(sum_blocks, shape((64, HEAD_DIM), F32), 1, 10**6, 10**6)(partial)
    return attended, grad_query, grad_key, grad_weight


def solution(mesh):
    fine = Mesh(mesh.devices.reshape(2, 4, 2, 8, 4), ("yh", "x", "core", "ctx", "mp"))
    tokens = P(("yh", "x", "core", "ctx"), "mp")
    return jax.shard_map(
        shards,
        mesh=fine,
        in_specs=(tokens,) * 5 + (P(("yh", "x", "core"), None),),
        out_specs=(tokens,) * 4,
        check_vma=False,
    )
```

```python
import jax
import jax.numpy as jnp
from jax import lax
from jax.experimental import pallas as pl
from jax.experimental.pallas import tpu as pltpu
from jax.sharding import Mesh, PartitionSpec as P

HEAD_DIM = 128
TOK = 192
GROUP = 8
REACH = 4
WINDOW = (REACH + 1) * TOK
HEADS_AT_ONCE = 2
LANES = HEADS_AT_ONCE * TOK
CHUNKS = GROUP // HEADS_AT_ONCE
CHIPS = ("yh", "x")
SCALE = HEAD_DIM ** -0.5
F32 = jnp.float32
BF16 = jnp.bfloat16
NT = (((1,), (1,)), ((), ()))
TN = (((0,), (0,)), ((), ()))
VMEM = pl.BlockSpec(memory_space=pltpu.VMEM)
SMEM = pl.BlockSpec(memory_space=pltpu.SMEM)


def shape(dims, dtype=BF16):
    return jax.ShapeDtypeStruct(dims, dtype)


def call(kernel, out_shape, n_in, flops, n_bytes, scratch=(), smem=0, vmem=48):
    outs = out_shape if isinstance(out_shape, tuple) else None
    return pl.pallas_call(
        kernel,
        out_shape=out_shape,
        in_specs=[SMEM] * smem + [VMEM] * n_in,
        out_specs=(VMEM,) * len(outs) if outs else VMEM,
        scratch_shapes=scratch,
        compiler_params=pltpu.CompilerParams(vmem_limit_bytes=vmem * 2**20),
        cost_estimate=pl.CostEstimate(
            flops=flops, bytes_accessed=n_bytes, transcendentals=0
        ),
        name=kernel.__name__,
    )


def to_all(block, axes, copies):
    return lax.all_to_all(
        jnp.broadcast_to(block[None], (copies,) + block.shape), axes, 0, 0, tiled=True
    )


def from_behind(block, distance):
    return lax.ppermute(block, "ctx", [(i, i + distance) for i in range(8 - distance)])


def from_ahead(block, distance):
    return lax.ppermute(block, "ctx", [(i + distance, i) for i in range(8 - distance)])


def weight_rows(w_ref, j):
    return jnp.concatenate([w_ref[ctx, j] for ctx in range(8)], axis=0)


def feature_columns(x_ref, j, core):
    place = pl.multiple_of(((j % 2) * 2 + core) * 512, 512)
    return x_ref[j // 2, :, pl.ds(place, 512)]


def project(x_ref, own_ref, other_ref, out_ref):
    core = lax.axis_index("core")
    total = jnp.zeros((TOK, HEAD_DIM), F32)
    for w_ref, half in ((own_ref, core), (other_ref, 1 - core)):
        for j in range(8):
            total += jnp.dot(
                feature_columns(x_ref, j, half), weight_rows(w_ref, j), preferred_element_type=F32
            )
    out_ref[...] = total.astype(BF16)


def weight_grad(x_ref, *refs):
    dv_refs, out_refs = refs[:5], refs[5:]
    core = lax.axis_index("core")
    dv = dv_refs[0][...]
    for ref in dv_refs[1:]:
        dv = dv + ref[...].astype(F32)
    dv = dv.astype(BF16)
    for out_ref, half in zip(out_refs, (core, 1 - core)):
        for j in range(8):
            rows = lax.dot_general(
                feature_columns(x_ref, j, half), dv, TN, preferred_element_type=F32
            ).astype(BF16)
            for ctx in range(8):
                out_ref[j, ctx] = rows[ctx * 64 : (ctx + 1) * 64]


def add_halves(a_ref, b_ref, out_ref):
    out_ref[...] = (a_ref[...].astype(F32) + b_ref[...].astype(F32)).astype(BF16)


def sum_blocks(parts_ref, out_ref):
    total = parts_ref[0].astype(F32)
    for i in range(1, parts_ref.shape[0]):
        total = total + parts_ref[i].astype(F32)
    out_ref[...] = total.astype(out_ref.dtype)


def rows_of_heads(wide_ref, rows_ref):
    for h in range(GROUP):
        rows_ref[h * TOK : (h + 1) * TOK] = wide_ref[:, h * HEAD_DIM : (h + 1) * HEAD_DIM]


def fill_bias(len_ref, bias):
    ctx = lax.axis_index("ctx")
    lane = lax.broadcasted_iota(jnp.int32, (1, LANES), 1)
    query = ctx * TOK + lax.rem(lane, TOK)
    first = jnp.zeros_like(query)
    end = jnp.int32(0)
    for d in range(8):
        end = end + len_ref[0, d]
        first = jnp.where(query >= end, end, first)
    offset = lax.broadcasted_iota(jnp.int32, (TOK, LANES), 0)
    for slot in range(REACH + 1):
        key = lax.rem(ctx - (REACH - slot) + 8, 8) * TOK + offset
        bias[slot * TOK : (slot + 1) * TOK] = jnp.where(
            (key >= first) & (key <= query), F32(0.0), F32(-1e30)
        )


def soft(len_ref, q_ref, do_ref, *refs):
    k_refs, dv_refs, stat_ref = refs[:5], refs[5:10], refs[10]
    q_rows, do_rows, bias, probs, keys = refs[11:]
    rows_of_heads(q_ref, q_rows)
    rows_of_heads(do_ref, do_rows)
    for slot, ref in enumerate(k_refs):
        keys[slot * TOK : (slot + 1) * TOK] = ref[...]
    fill_bias(len_ref, bias)
    for i in range(CHUNKS):
        cols = slice(i * LANES, (i + 1) * LANES)
        scores = lax.dot_general(keys[...], q_rows[cols], NT, preferred_element_type=F32)
        scores = scores * F32(SCALE) + bias[...]
        top = jnp.max(scores, axis=0, keepdims=True)
        weights = jnp.exp(scores - top)
        inverse = 1.0 / jnp.sum(weights, axis=0, keepdims=True)
        probs[:, cols] = (weights * inverse).astype(BF16)
        stat_ref[i : i + 1] = top
        stat_ref[CHUNKS + i : CHUNKS + i + 1] = inverse
    total = jnp.dot(probs[...], do_rows[...], preferred_element_type=F32)
    for slot, ref in enumerate(dv_refs):
        ref[...] = total[slot * TOK : (slot + 1) * TOK].astype(ref.dtype)


def attend(len_ref, q_ref, do_ref, stat_ref, *refs):
    k_refs, v_refs, (att_ref, dq_ref), dk_refs = refs[:5], refs[5:10], refs[10:12], refs[12:17]
    q_rows, do_rows, bias, dscores, keys, values = refs[17:]
    rows_of_heads(q_ref, q_rows)
    rows_of_heads(do_ref, do_rows)
    for slot in range(REACH + 1):
        keys[slot * TOK : (slot + 1) * TOK] = k_refs[slot][...]
        values[slot * TOK : (slot + 1) * TOK] = v_refs[slot][...]
    fill_bias(len_ref, bias)
    for i in range(CHUNKS):
        cols = slice(i * LANES, (i + 1) * LANES)
        scores = lax.dot_general(keys[...], q_rows[cols], NT, preferred_element_type=F32)
        scores = scores * F32(SCALE) + bias[...]
        p = jnp.exp(scores - stat_ref[i : i + 1]) * stat_ref[CHUNKS + i : CHUNKS + i + 1]
        att = lax.dot_general(values[...], p.astype(BF16), TN, preferred_element_type=F32)
        dp = lax.dot_general(values[...], do_rows[cols], NT, preferred_element_type=F32)
        dots = jnp.sum(p * dp, axis=0, keepdims=True)
        ds = (p * (dp - dots)).astype(BF16)
        dscores[:, cols] = ds
        dq = lax.dot_general(keys[...], ds, TN, preferred_element_type=F32) * F32(SCALE)
        att = att.T.astype(BF16)
        dq = dq.T.astype(BF16)
        for j in range(HEADS_AT_ONCE):
            head = slice((i * HEADS_AT_ONCE + j) * HEAD_DIM, (i * HEADS_AT_ONCE + j + 1) * HEAD_DIM)
            att_ref[:, head] = att[j * TOK : (j + 1) * TOK]
            dq_ref[:, head] = dq[j * TOK : (j + 1) * TOK]
    total = jnp.dot(dscores[...], q_rows[...], preferred_element_type=F32)
    for slot, ref in enumerate(dk_refs):
        ref[...] = total[slot * TOK : (slot + 1) * TOK].astype(ref.dtype)


def shards(queries, key_states, normed, value_weight, grad_out, lengths):
    features = lax.all_gather(normed, "mp", axis=0)
    keys = [from_behind(key_states, d) for d in range(REACH, 0, -1)] + [key_states]
    chips = to_all(value_weight, CHIPS, 8)
    spread = jnp.broadcast_to(chips[None], (8, 8, 64, HEAD_DIM))
    spread, keys = lax.optimization_barrier((spread, keys))

    weight = lax.all_to_all(spread, "ctx", 0, 0, tiled=True)
    heads = GROUP * TOK
    rows = pltpu.VMEM((heads, HEAD_DIM), BF16)
    window = pltpu.VMEM((WINDOW, HEAD_DIM), BF16)
    bias = pltpu.VMEM((WINDOW, LANES), F32)
    pairs = pltpu.VMEM((WINDOW, heads), BF16)
    block = shape((TOK, HEAD_DIM))
    own = shape((TOK, HEAD_DIM), F32)
    whole = shape((8, 8, 64, HEAD_DIM))
    *dv, stats = call(
        soft, (block,) * REACH + (own, shape((8, LANES), F32)), 7, 3 * 10**9, 2 * 10**6,
        (rows, rows, bias, pairs, window), smem=1, vmem=56,
    )(lengths, queries, grad_out, *keys)
    dv = [dv[REACH]] + [from_ahead(dv[REACH - d], d) for d in range(1, REACH + 1)]

    weight, dv = lax.optimization_barrier((weight, dv))
    other = lax.ppermute(weight, "core", [(0, 1), (1, 0)])
    other, dv = lax.optimization_barrier((other, dv))

    partial, given = call(weight_grad, (whole, whole), 6, 4 * 10**8, 5 * 10**6)(features, *dv)
    taken = lax.ppermute(given, "core", [(0, 1), (1, 0)])
    projected = call(project, block, 3, 4 * 10**8, 5 * 10**6)(features, weight, other)
    taken, projected = lax.optimization_barrier((taken, projected))
    values = [from_behind(projected, d) for d in range(REACH, 0, -1)] + [projected]
    partial = call(add_halves, whole, 2, 10**6, 3 * 10**6)(partial, taken)
    partial = lax.all_to_all(partial, CHIPS, 0, 0, tiled=True)

    wide = shape((TOK, GROUP * HEAD_DIM))
    attended, grad_query, *dk = call(
        attend, (wide, wide) + (block,) * REACH + (own,), 13, 6 * 10**9, 4 * 10**6,
        (rows, rows, bias, pairs, window, window), smem=1, vmem=56,
    )(lengths, queries, grad_out, stats, *keys, *values)
    partial, dk = lax.optimization_barrier((partial, dk))
    dk = [dk[REACH]] + [from_ahead(dk[REACH - d], d) for d in range(1, REACH + 1)]
    grad_key = (sum(part.astype(F32) for part in dk) * F32(SCALE)).astype(BF16)

    partial = call(sum_blocks, shape((8, 64, HEAD_DIM)), 1, 10**6, 10**6)(partial)
    partial = lax.all_to_all(partial, "ctx", 0, 0, tiled=True)
    grad_weight = call(sum_blocks, shape((64, HEAD_DIM), F32), 1, 10**6, 10**6)(partial)
    return attended, grad_query, grad_key, grad_weight


def solution(mesh):
    fine = Mesh(mesh.devices.reshape(2, 4, 2, 8, 4), ("yh", "x", "core", "ctx", "mp"))
    tokens = P(("yh", "x", "core", "ctx"), "mp")
    return jax.shard_map(
        shards,
        mesh=fine,
        in_specs=(tokens,) * 5 + (P(("yh", "x", "core"), None),),
        out_specs=(tokens,) * 4,
        check_vma=False,
    )
```

```python
import jax
import jax.numpy as jnp
from jax import lax
from jax.experimental import pallas as pl
from jax.experimental.pallas import tpu as pltpu
from jax.sharding import Mesh, PartitionSpec as P

HEAD_DIM = 128
TOK = 192
GROUP = 8
REACH = 4
WINDOW = (REACH + 1) * TOK
HEADS_AT_ONCE = 2
LANES = HEADS_AT_ONCE * TOK
CHUNKS = GROUP // HEADS_AT_ONCE
CHIPS = ("yh", "x")
SCALE = HEAD_DIM ** -0.5
F32 = jnp.float32
BF16 = jnp.bfloat16
NT = (((1,), (1,)), ((), ()))
TN = (((0,), (0,)), ((), ()))
VMEM = pl.BlockSpec(memory_space=pltpu.VMEM)
SMEM = pl.BlockSpec(memory_space=pltpu.SMEM)


def shape(dims, dtype=BF16):
    return jax.ShapeDtypeStruct(dims, dtype)


def call(kernel, out_shape, n_in, flops, n_bytes, scratch=(), smem=0, vmem=48):
    outs = out_shape if isinstance(out_shape, tuple) else None
    return pl.pallas_call(
        kernel,
        out_shape=out_shape,
        in_specs=[SMEM] * smem + [VMEM] * n_in,
        out_specs=(VMEM,) * len(outs) if outs else VMEM,
        scratch_shapes=scratch,
        compiler_params=pltpu.CompilerParams(vmem_limit_bytes=vmem * 2**20),
        cost_estimate=pl.CostEstimate(
            flops=flops, bytes_accessed=n_bytes, transcendentals=0
        ),
        name=kernel.__name__,
    )


def to_all(block, axes, copies):
    return lax.all_to_all(
        jnp.broadcast_to(block[None], (copies,) + block.shape), axes, 0, 0, tiled=True
    )


def from_behind(block, distance):
    return lax.ppermute(block, "ctx", [(i, i + distance) for i in range(8 - distance)])


def from_ahead(block, distance):
    return lax.ppermute(block, "ctx", [(i + distance, i) for i in range(8 - distance)])


def weight_rows(w_ref, j):
    return jnp.concatenate([w_ref[ctx, j] for ctx in range(8)], axis=0)


def feature_columns(x_ref, j, core):
    place = pl.multiple_of(((j % 2) * 2 + core) * 512, 512)
    return x_ref[j // 2, :, pl.ds(place, 512)]


def project(x_ref, own_ref, other_ref, out_ref):
    core = lax.axis_index("core")
    total = jnp.zeros((TOK, HEAD_DIM), F32)
    for w_ref, half in ((own_ref, core), (other_ref, 1 - core)):
        for j in range(8):
            total += jnp.dot(
                feature_columns(x_ref, j, half), weight_rows(w_ref, j), preferred_element_type=F32
            )
    out_ref[...] = total.astype(BF16)


def weight_grad(x_ref, *refs):
    dv_refs, out_refs = refs[:5], refs[5:]
    core = lax.axis_index("core")
    dv = dv_refs[0][...]
    for ref in dv_refs[1:]:
        dv = dv + ref[...].astype(F32)
    dv = dv.astype(BF16)
    for out_ref, half in zip(out_refs, (core, 1 - core)):
        for j in range(8):
            rows = lax.dot_general(
                feature_columns(x_ref, j, half), dv, TN, preferred_element_type=F32
            ).astype(BF16)
            for ctx in range(8):
                out_ref[j, ctx] = rows[ctx * 64 : (ctx + 1) * 64]


def add_halves(a_ref, b_ref, out_ref):
    out_ref[...] = (a_ref[...].astype(F32) + b_ref[...].astype(F32)).astype(BF16)


def sum_of(parts):
    total = parts[0].astype(F32)
    for part in parts[1:]:
        total = total + part.astype(F32)
    return total


def pack(parts_ref, dk_ref, out_ref):
    for ctx in range(8):
        out_ref[ctx, :64] = sum_of([parts_ref[i, ctx] for i in range(8)]).astype(BF16)
        out_ref[ctx, 64:] = dk_ref[ctx]


def unpack(parts_ref, weight_ref, key_ref):
    weight_ref[...] = sum_of([parts_ref[i, :64] for i in range(8)])
    key_ref[...] = (sum_of([parts_ref[i, 64:] for i in range(8)]) * F32(SCALE)).astype(BF16)


def rows_of_heads(wide_ref, rows_ref):
    for h in range(GROUP):
        rows_ref[h * TOK : (h + 1) * TOK] = wide_ref[:, h * HEAD_DIM : (h + 1) * HEAD_DIM]


def slot_owner(slot):
    return lax.rem(lax.axis_index("ctx") - (REACH - slot) + 8, 8)


def fill_bias(len_ref, bias):
    ctx = lax.axis_index("ctx")
    lane = lax.broadcasted_iota(jnp.int32, (1, LANES), 1)
    query = ctx * TOK + lax.rem(lane, TOK)
    first = jnp.zeros_like(query)
    end = jnp.int32(0)
    for d in range(8):
        end = end + len_ref[0, d]
        first = jnp.where(query >= end, end, first)
    offset = lax.broadcasted_iota(jnp.int32, (TOK, LANES), 0)
    for slot in range(REACH + 1):
        key = slot_owner(slot) * TOK + offset
        bias[slot * TOK : (slot + 1) * TOK] = jnp.where(
            (key >= first) & (key <= query), F32(0.0), F32(-1e30)
        )


def soft(len_ref, q_ref, do_ref, *refs):
    k_refs, dv_refs, stat_ref = refs[:5], refs[5:10], refs[10]
    q_rows, do_rows, bias, probs, keys = refs[11:]
    rows_of_heads(q_ref, q_rows)
    rows_of_heads(do_ref, do_rows)
    for slot, ref in enumerate(k_refs):
        keys[slot * TOK : (slot + 1) * TOK] = ref[...]
    fill_bias(len_ref, bias)
    for i in range(CHUNKS):
        cols = slice(i * LANES, (i + 1) * LANES)
        scores = lax.dot_general(keys[...], q_rows[cols], NT, preferred_element_type=F32)
        scores = scores * F32(SCALE) + bias[...]
        top = jnp.max(scores, axis=0, keepdims=True)
        weights = jnp.exp(scores - top)
        inverse = 1.0 / jnp.sum(weights, axis=0, keepdims=True)
        probs[:, cols] = (weights * inverse).astype(BF16)
        stat_ref[i : i + 1] = top
        stat_ref[CHUNKS + i : CHUNKS + i + 1] = inverse
    total = jnp.dot(probs[...], do_rows[...], preferred_element_type=F32)
    for slot, ref in enumerate(dv_refs):
        ref[...] = total[slot * TOK : (slot + 1) * TOK].astype(ref.dtype)


def attend(len_ref, q_ref, do_ref, stat_ref, *refs):
    k_refs, v_refs, (att_ref, dq_ref, dk_ref) = refs[:5], refs[5:10], refs[10:13]
    q_rows, do_rows, bias, dscores, keys, values = refs[13:]
    rows_of_heads(q_ref, q_rows)
    rows_of_heads(do_ref, do_rows)
    for slot in range(REACH + 1):
        keys[slot * TOK : (slot + 1) * TOK] = k_refs[slot][...]
        values[slot * TOK : (slot + 1) * TOK] = v_refs[slot][...]
    fill_bias(len_ref, bias)
    for i in range(CHUNKS):
        cols = slice(i * LANES, (i + 1) * LANES)
        scores = lax.dot_general(keys[...], q_rows[cols], NT, preferred_element_type=F32)
        scores = scores * F32(SCALE) + bias[...]
        p = jnp.exp(scores - stat_ref[i : i + 1]) * stat_ref[CHUNKS + i : CHUNKS + i + 1]
        att = lax.dot_general(values[...], p.astype(BF16), TN, preferred_element_type=F32)
        dp = lax.dot_general(values[...], do_rows[cols], NT, preferred_element_type=F32)
        dots = jnp.sum(p * dp, axis=0, keepdims=True)
        ds = (p * (dp - dots)).astype(BF16)
        dscores[:, cols] = ds
        dq = lax.dot_general(keys[...], ds, TN, preferred_element_type=F32) * F32(SCALE)
        att = att.T.astype(BF16)
        dq = dq.T.astype(BF16)
        for j in range(HEADS_AT_ONCE):
            head = slice((i * HEADS_AT_ONCE + j) * HEAD_DIM, (i * HEADS_AT_ONCE + j + 1) * HEAD_DIM)
            att_ref[:, head] = att[j * TOK : (j + 1) * TOK]
            dq_ref[:, head] = dq[j * TOK : (j + 1) * TOK]
    total = jnp.dot(dscores[...], q_rows[...], preferred_element_type=F32).astype(BF16)
    dk_ref[...] = jnp.zeros_like(dk_ref)
    for slot in range(REACH + 1):
        dk_ref[slot_owner(slot)] = total[slot * TOK : (slot + 1) * TOK]


def shards(queries, key_states, normed, value_weight, grad_out, lengths):
    features = lax.all_gather(normed, "mp", axis=0)
    keys = [from_behind(key_states, d) for d in range(REACH, 0, -1)] + [key_states]
    chips = to_all(value_weight, CHIPS, 8)
    spread = jnp.broadcast_to(chips[None], (8, 8, 64, HEAD_DIM))
    spread, keys = lax.optimization_barrier((spread, keys))

    weight = lax.all_to_all(spread, "ctx", 0, 0, tiled=True)
    heads = GROUP * TOK
    rows = pltpu.VMEM((heads, HEAD_DIM), BF16)
    window = pltpu.VMEM((WINDOW, HEAD_DIM), BF16)
    bias = pltpu.VMEM((WINDOW, LANES), F32)
    pairs = pltpu.VMEM((WINDOW, heads), BF16)
    block = shape((TOK, HEAD_DIM))
    own = shape((TOK, HEAD_DIM), F32)
    whole = shape((8, 8, 64, HEAD_DIM))
    *dv, stats = call(
        soft, (block,) * REACH + (own, shape((8, LANES), F32)), 7, 3 * 10**9, 2 * 10**6,
        (rows, rows, bias, pairs, window), smem=1, vmem=56,
    )(lengths, queries, grad_out, *keys)
    dv = [dv[REACH]] + [from_ahead(dv[REACH - d], d) for d in range(1, REACH + 1)]

    weight, dv = lax.optimization_barrier((weight, dv))
    other = lax.ppermute(weight, "core", [(0, 1), (1, 0)])
    other, dv = lax.optimization_barrier((other, dv))

    partial, given = call(weight_grad, (whole, whole), 6, 4 * 10**8, 5 * 10**6)(features, *dv)
    taken = lax.ppermute(given, "core", [(0, 1), (1, 0)])
    projected = call(project, block, 3, 4 * 10**8, 5 * 10**6)(features, weight, other)
    taken, projected = lax.optimization_barrier((taken, projected))
    values = [from_behind(projected, d) for d in range(REACH, 0, -1)] + [projected]
    partial = call(add_halves, whole, 2, 10**6, 3 * 10**6)(partial, taken)
    partial = lax.all_to_all(partial, CHIPS, 0, 0, tiled=True)

    wide = shape((TOK, GROUP * HEAD_DIM))
    attended, grad_query, dk = call(
        attend, (wide, wide, shape((8, TOK, HEAD_DIM))), 13, 6 * 10**9, 4 * 10**6,
        (rows, rows, bias, pairs, window, window), smem=1, vmem=56,
    )(lengths, queries, grad_out, stats, *keys, *values)
    parts = call(pack, shape((8, 64 + TOK, HEAD_DIM)), 2, 10**6, 2 * 10**6)(partial, dk)
    parts = lax.all_to_all(parts, "ctx", 0, 0, tiled=True)
    grad_weight, grad_key = call(
        unpack, (shape((64, HEAD_DIM), F32), block), 1, 10**6, 10**6
    )(parts)
    return attended, grad_query, grad_key, grad_weight


def solution(mesh):
    fine = Mesh(mesh.devices.reshape(2, 4, 2, 8, 4), ("yh", "x", "core", "ctx", "mp"))
    tokens = P(("yh", "x", "core", "ctx"), "mp")
    return jax.shard_map(
        shards,
        mesh=fine,
        in_specs=(tokens,) * 5 + (P(("yh", "x", "core"), None),),
        out_specs=(tokens,) * 4,
        check_vma=False,
    )
```

```python
import jax
import jax.numpy as jnp
from jax import lax
from jax.experimental import pallas as pl
from jax.experimental.pallas import tpu as pltpu
from jax.sharding import Mesh, PartitionSpec as P

HEAD_DIM = 128
TOK = 192
GROUP = 8
REACH = 4
WINDOW = (REACH + 1) * TOK
HEADS_AT_ONCE = 2
LANES = HEADS_AT_ONCE * TOK
CHUNKS = GROUP // HEADS_AT_ONCE
PAIR = [(0, 1), (1, 0)]
SCALE = HEAD_DIM ** -0.5
F32 = jnp.float32
BF16 = jnp.bfloat16
NT = (((1,), (1,)), ((), ()))
TN = (((0,), (0,)), ((), ()))
VMEM = pl.BlockSpec(memory_space=pltpu.VMEM)
SMEM = pl.BlockSpec(memory_space=pltpu.SMEM)


def shape(dims, dtype=BF16):
    return jax.ShapeDtypeStruct(dims, dtype)


def call(kernel, out_shape, n_in, flops, n_bytes, scratch=(), smem=0, vmem=48):
    outs = out_shape if isinstance(out_shape, tuple) else None
    return pl.pallas_call(
        kernel,
        out_shape=out_shape,
        in_specs=[SMEM] * smem + [VMEM] * n_in,
        out_specs=(VMEM,) * len(outs) if outs else VMEM,
        scratch_shapes=scratch,
        compiler_params=pltpu.CompilerParams(vmem_limit_bytes=vmem * 2**20),
        cost_estimate=pl.CostEstimate(
            flops=flops, bytes_accessed=n_bytes, transcendentals=0
        ),
        name=kernel.__name__,
    )


def to_all(block, axes, copies):
    return lax.all_to_all(
        jnp.broadcast_to(block[None], (copies,) + block.shape), axes, 0, 0, tiled=True
    )


def from_behind(block, distance):
    return lax.ppermute(block, "ctx", [(i, i + distance) for i in range(8 - distance)])


def from_ahead(block, distance):
    return lax.ppermute(block, "ctx", [(i + distance, i) for i in range(8 - distance)])


def feature_steps(own_ref, near_ref, half):
    m0 = lax.axis_index("m0")
    for step in range(4):
        ref, m = (own_ref, m0) if step < 2 else (near_ref, 1 - m0)
        place = pl.multiple_of((step % 2) * 1024 + half * 512, 512)
        yield ref[:, pl.ds(place, 512)], 2 * m + step % 2


def project(own_ref, near_ref, mine_ref, other_ref, keep_ref, give_ref):
    core, m1 = lax.axis_index("core"), lax.axis_index("m1")
    total = jnp.zeros((TOK, 2 * HEAD_DIM), F32)
    for w_ref, half in ((mine_ref, core), (other_ref, 1 - core)):
        for columns, x in feature_steps(own_ref, near_ref, half):
            weight = jnp.concatenate(
                [
                    jnp.concatenate([w_ref[x, ctx, c] for c in range(2)], axis=1)
                    for ctx in range(8)
                ],
                axis=0,
            )
            total += jnp.dot(columns, weight, preferred_element_type=F32)
    low, high = total[:, :HEAD_DIM], total[:, HEAD_DIM:]
    keep_ref[...] = jnp.where(m1 == 0, low, high)
    give_ref[...] = jnp.where(m1 == 0, high, low).astype(BF16)


def weight_grad(own_ref, near_ref, dv_ref, far_dv_ref, *out_refs):
    core, m1 = lax.axis_index("core"), lax.axis_index("m1")
    mine, far = dv_ref[...], far_dv_ref[...]
    dv = jnp.concatenate([jnp.where(m1 == 0, mine, far), jnp.where(m1 == 0, far, mine)], axis=1)
    for out_ref, half in zip(out_refs, (core, 1 - core)):
        for columns, x in feature_steps(own_ref, near_ref, half):
            rows = lax.dot_general(columns, dv, TN, preferred_element_type=F32).astype(BF16)
            for ctx in range(8):
                for c in range(2):
                    out_ref[x, ctx, c] = rows[
                        ctx * 64 : (ctx + 1) * 64, c * HEAD_DIM : (c + 1) * HEAD_DIM
                    ]


def add_halves(a_ref, b_ref, out_ref):
    out_ref[...] = (a_ref[...].astype(F32) + b_ref[...].astype(F32)).astype(BF16)


def sum_of(parts):
    total = parts[0].astype(F32)
    for part in parts[1:]:
        total = total + part.astype(F32)
    return total


def sum_blocks(parts_ref, out_ref):
    out_ref[...] = sum_of([parts_ref[i] for i in range(parts_ref.shape[0])]).astype(out_ref.dtype)


def twice_sum(parts_ref, out_ref):
    total = sum_of([parts_ref[i] for i in range(8)])
    for i in range(2):
        out_ref[i] = total


def rows_of_heads(wide_ref, rows_ref):
    for h in range(GROUP):
        rows_ref[h * TOK : (h + 1) * TOK] = wide_ref[:, h * HEAD_DIM : (h + 1) * HEAD_DIM]


def slot_owner(slot):
    return lax.rem(lax.axis_index("ctx") - (REACH - slot) + 8, 8)


def fill_bias(len_ref, bias):
    ctx = lax.axis_index("ctx")
    lane = lax.broadcasted_iota(jnp.int32, (1, LANES), 1)
    query = ctx * TOK + lax.rem(lane, TOK)
    first = jnp.zeros_like(query)
    end = jnp.int32(0)
    for d in range(8):
        end = end + len_ref[0, d]
        first = jnp.where(query >= end, end, first)
    offset = lax.broadcasted_iota(jnp.int32, (TOK, LANES), 0)
    for slot in range(REACH + 1):
        key = slot_owner(slot) * TOK + offset
        bias[slot * TOK : (slot + 1) * TOK] = jnp.where(
            (key >= first) & (key <= query), F32(0.0), F32(-1e30)
        )


def soft(len_ref, q_ref, do_ref, *refs):
    k_refs, dv_refs, stat_ref = refs[:5], refs[5:10], refs[10]
    q_rows, do_rows, bias, probs, keys = refs[11:]
    rows_of_heads(q_ref, q_rows)
    rows_of_heads(do_ref, do_rows)
    for slot, ref in enumerate(k_refs):
        keys[slot * TOK : (slot + 1) * TOK] = ref[...]
    fill_bias(len_ref, bias)
    for i in range(CHUNKS):
        cols = slice(i * LANES, (i + 1) * LANES)
        scores = lax.dot_general(keys[...], q_rows[cols], NT, preferred_element_type=F32)
        scores = scores * F32(SCALE) + bias[...]
        top = jnp.max(scores, axis=0, keepdims=True)
        weights = jnp.exp(scores - top)
        inverse = 1.0 / jnp.sum(weights, axis=0, keepdims=True)
        probs[:, cols] = (weights * inverse).astype(BF16)
        stat_ref[i : i + 1] = top
        stat_ref[CHUNKS + i : CHUNKS + i + 1] = inverse
    total = jnp.dot(probs[...], do_rows[...], preferred_element_type=F32)
    for slot, ref in enumerate(dv_refs):
        ref[...] = total[slot * TOK : (slot + 1) * TOK].astype(ref.dtype)


def attend(len_ref, q_ref, do_ref, stat_ref, *refs):
    k_refs, v_refs, (att_ref, dq_ref), dk_refs = refs[:5], refs[5:10], refs[10:12], refs[12:17]
    q_rows, do_rows, bias, dscores, keys, values = refs[17:]
    rows_of_heads(q_ref, q_rows)
    rows_of_heads(do_ref, do_rows)
    for slot in range(REACH + 1):
        keys[slot * TOK : (slot + 1) * TOK] = k_refs[slot][...]
        values[slot * TOK : (slot + 1) * TOK] = v_refs[slot][...]
    fill_bias(len_ref, bias)
    for i in range(CHUNKS):
        cols = slice(i * LANES, (i + 1) * LANES)
        scores = lax.dot_general(keys[...], q_rows[cols], NT, preferred_element_type=F32)
        scores = scores * F32(SCALE) + bias[...]
        p = jnp.exp(scores - stat_ref[i : i + 1]) * stat_ref[CHUNKS + i : CHUNKS + i + 1]
        att = lax.dot_general(values[...], p.astype(BF16), TN, preferred_element_type=F32)
        dp = lax.dot_general(values[...], do_rows[cols], NT, preferred_element_type=F32)
        dots = jnp.sum(p * dp, axis=0, keepdims=True)
        ds = (p * (dp - dots)).astype(BF16)
        dscores[:, cols] = ds
        dq = lax.dot_general(keys[...], ds, TN, preferred_element_type=F32) * F32(SCALE)
        att = att.T.astype(BF16)
        dq = dq.T.astype(BF16)
        for j in range(HEADS_AT_ONCE):
            head = slice((i * HEADS_AT_ONCE + j) * HEAD_DIM, (i * HEADS_AT_ONCE + j + 1) * HEAD_DIM)
            att_ref[:, head] = att[j * TOK : (j + 1) * TOK]
            dq_ref[:, head] = dq[j * TOK : (j + 1) * TOK]
    total = jnp.dot(dscores[...], q_rows[...], preferred_element_type=F32)
    for slot, ref in enumerate(dk_refs):
        ref[...] = total[slot * TOK : (slot + 1) * TOK].astype(ref.dtype)


def shards(queries, key_states, normed, value_weight, grad_out, lengths):
    yh, m1 = lax.axis_index("yh"), lax.axis_index("m1")
    corners = to_all(value_weight, ("yh", "m1"), 4)
    near = lax.ppermute(normed, "m0", PAIR)
    keys = [from_behind(key_states, d) for d in range(REACH, 0, -1)] + [key_states]
    corners, keys = lax.optimization_barrier((corners, keys))
    weight = to_all(lax.dynamic_slice_in_dim(corners, 2 * m1, 2, 0), "ctx", 8)
    heads = GROUP * TOK
    rows = pltpu.VMEM((heads, HEAD_DIM), BF16)
    window = pltpu.VMEM((WINDOW, HEAD_DIM), BF16)
    bias = pltpu.VMEM((WINDOW, LANES), F32)
    pairs = pltpu.VMEM((WINDOW, heads), BF16)
    block = shape((TOK, HEAD_DIM))
    own = shape((TOK, HEAD_DIM), F32)
    whole = shape((4, 8, 2, 64, HEAD_DIM))
    *dv, stats = call(
        soft, (block,) * REACH + (own, shape((8, LANES), F32)), 7, 3 * 10**9, 2 * 10**6,
        (rows, rows, bias, pairs, window), smem=1, vmem=56,
    )(lengths, queries, grad_out, *keys)
    weight, stats = lax.optimization_barrier((weight, stats))
    weight = to_all(weight, "x", 4)
    dv = [dv[REACH]] + [from_ahead(dv[REACH - d], d) for d in range(1, REACH + 1)]
    dv = sum_of(dv).astype(BF16)
    far_dv = lax.ppermute(dv, "m1", PAIR)
    other = lax.ppermute(weight, "core", PAIR)

    partial, given = call(weight_grad, (whole, whole), 4, 4 * 10**8, 5 * 10**6)(
        normed, near, dv, far_dv
    )
    taken = lax.ppermute(given, "core", PAIR)
    kept, given = call(project, (own, block), 4, 4 * 10**8, 5 * 10**6)(normed, near, weight, other)
    projected = (kept + lax.ppermute(given, "m1", PAIR).astype(F32)).astype(BF16)
    values = [from_behind(projected, d) for d in range(REACH, 0, -1)] + [projected]
    partial = call(add_halves, whole, 2, 10**6, 3 * 10**6)(partial, taken)
    partial = lax.all_to_all(partial, "x", 0, 0, tiled=True)
    partial = call(sum_blocks, shape((8, 2, 64, HEAD_DIM)), 1, 10**6, 10**6)(partial)
    partial, values = lax.optimization_barrier((partial, values))
    partial = lax.all_to_all(partial, "ctx", 0, 0, tiled=True)

    wide = shape((TOK, GROUP * HEAD_DIM))
    attended, grad_query, *dk = call(
        attend, (wide, wide) + (block,) * REACH + (own,), 13, 6 * 10**9, 4 * 10**6,
        (rows, rows, bias, pairs, window, window), smem=1, vmem=56,
    )(lengths, queries, grad_out, stats, *keys, *values)
    partial = call(twice_sum, shape((2, 2, 64, HEAD_DIM), F32), 1, 10**6, 10**6)(partial)
    partial, dk = lax.optimization_barrier((partial, dk))
    partial = lax.all_to_all(partial.reshape(4, 64, HEAD_DIM), ("yh", "m1"), 0, 0, tiled=True)
    grad_weight = jnp.sum(
        lax.dynamic_index_in_dim(
            partial.reshape(2, 2, 64, HEAD_DIM), yh, axis=1, keepdims=False
        ),
        axis=0,
    )
    dk = [dk[REACH]] + [from_ahead(dk[REACH - d], d) for d in range(1, REACH + 1)]
    grad_key = (sum(part.astype(F32) for part in dk) * F32(SCALE)).astype(BF16)
    return attended, grad_query, grad_key, grad_weight


def solution(mesh):
    axes = ("yh", "x", "core", "ctx", "m1", "m0")
    fine = Mesh(mesh.devices.reshape(2, 4, 2, 8, 2, 2), axes)
    tokens = P(axes[:4], axes[4:])
    return jax.shard_map(
        shards,
        mesh=fine,
        in_specs=(tokens,) * 5 + (P(axes[:3], None),),
        out_specs=(tokens,) * 4,
        check_vma=False,
    )
```

```python
import jax
import jax.numpy as jnp
from jax import lax
from jax.experimental import pallas as pl
from jax.experimental.pallas import tpu as pltpu
from jax.sharding import Mesh, PartitionSpec as P

HEAD_DIM = 128
TOK = 192
GROUP = 8
REACH = 4
WINDOW = (REACH + 1) * TOK
HEADS_AT_ONCE = 2
LANES = HEADS_AT_ONCE * TOK
CHUNKS = GROUP // HEADS_AT_ONCE
PAIR = [(0, 1), (1, 0)]
SCALE = HEAD_DIM ** -0.5
F32 = jnp.float32
BF16 = jnp.bfloat16
NT = (((1,), (1,)), ((), ()))
TN = (((0,), (0,)), ((), ()))
VMEM = pl.BlockSpec(memory_space=pltpu.VMEM)
SMEM = pl.BlockSpec(memory_space=pltpu.SMEM)


def shape(dims, dtype=BF16):
    return jax.ShapeDtypeStruct(dims, dtype)


def call(kernel, out_shape, n_in, flops, n_bytes, scratch=(), smem=0, vmem=20):
    outs = out_shape if isinstance(out_shape, tuple) else None
    return pl.pallas_call(
        kernel,
        out_shape=out_shape,
        in_specs=[SMEM] * smem + [VMEM] * n_in,
        out_specs=(VMEM,) * len(outs) if outs else VMEM,
        scratch_shapes=scratch,
        compiler_params=pltpu.CompilerParams(vmem_limit_bytes=vmem * 2**20),
        cost_estimate=pl.CostEstimate(
            flops=flops, bytes_accessed=n_bytes, transcendentals=0
        ),
        name=kernel.__name__,
    )


def to_all(block, axes, copies):
    return lax.all_to_all(
        jnp.broadcast_to(block[None], (copies,) + block.shape), axes, 0, 0, tiled=True
    )


def from_behind(block, distance):
    return lax.ppermute(block, "ctx", [(i, i + distance) for i in range(8 - distance)])


def from_ahead(block, distance):
    return lax.ppermute(block, "ctx", [(i + distance, i) for i in range(8 - distance)])


def feature_steps(own_ref, near_ref, half):
    m0 = lax.axis_index("m0")
    for step in range(4):
        ref, m = (own_ref, m0) if step < 2 else (near_ref, 1 - m0)
        place = pl.multiple_of((step % 2) * 1024 + half * 512, 512)
        yield ref[:, pl.ds(place, 512)], 2 * m + step % 2


def project(own_ref, near_ref, mine_ref, other_ref, keep_ref, give_ref):
    core, m1 = lax.axis_index("core"), lax.axis_index("m1")
    total = jnp.zeros((TOK, 2 * HEAD_DIM), F32)
    for w_ref, half in ((mine_ref, core), (other_ref, 1 - core)):
        for columns, x in feature_steps(own_ref, near_ref, half):
            weight = jnp.concatenate(
                [
                    jnp.concatenate([w_ref[x, ctx, c] for c in range(2)], axis=1)
                    for ctx in range(8)
                ],
                axis=0,
            )
            total += jnp.dot(columns, weight, preferred_element_type=F32)
    low, high = total[:, :HEAD_DIM], total[:, HEAD_DIM:]
    keep_ref[...] = jnp.where(m1 == 0, low, high)
    give_ref[...] = jnp.where(m1 == 0, high, low).astype(BF16)


def weight_grad(own_ref, near_ref, dv_ref, far_dv_ref, *out_refs):
    core, m1 = lax.axis_index("core"), lax.axis_index("m1")
    mine, far = dv_ref[...], far_dv_ref[...]
    dv = jnp.concatenate([jnp.where(m1 == 0, mine, far), jnp.where(m1 == 0, far, mine)], axis=1)
    for out_ref, half in zip(out_refs, (core, 1 - core)):
        for columns, x in feature_steps(own_ref, near_ref, half):
            rows = lax.dot_general(columns, dv, TN, preferred_element_type=F32).astype(BF16)
            for ctx in range(8):
                for c in range(2):
                    out_ref[x, ctx, c] = rows[
                        ctx * 64 : (ctx + 1) * 64, c * HEAD_DIM : (c + 1) * HEAD_DIM
                    ]


def add_halves(a_ref, b_ref, out_ref):
    out_ref[...] = (a_ref[...].astype(F32) + b_ref[...].astype(F32)).astype(BF16)


def sum_of(parts):
    total = parts[0].astype(F32)
    for part in parts[1:]:
        total = total + part.astype(F32)
    return total


def sum_blocks(parts_ref, out_ref):
    out_ref[...] = sum_of([parts_ref[i] for i in range(parts_ref.shape[0])]).astype(out_ref.dtype)


def twice_sum(parts_ref, out_ref):
    total = sum_of([parts_ref[i] for i in range(8)])
    for i in range(2):
        out_ref[i] = total


def rows_of_heads(wide_ref, rows_ref):
    for h in range(GROUP):
        rows_ref[h * TOK : (h + 1) * TOK] = wide_ref[:, h * HEAD_DIM : (h + 1) * HEAD_DIM]


def slot_owner(slot):
    return lax.rem(lax.axis_index("ctx") - (REACH - slot) + 8, 8)


def fill_bias(len_ref, bias):
    ctx = lax.axis_index("ctx")
    lane = lax.broadcasted_iota(jnp.int32, (1, LANES), 1)
    query = ctx * TOK + lax.rem(lane, TOK)
    first = jnp.zeros_like(query)
    end = jnp.int32(0)
    for d in range(8):
        end = end + len_ref[0, d]
        first = jnp.where(query >= end, end, first)
    offset = lax.broadcasted_iota(jnp.int32, (TOK, LANES), 0)
    for slot in range(REACH + 1):
        key = slot_owner(slot) * TOK + offset
        bias[slot * TOK : (slot + 1) * TOK] = jnp.where(
            (key >= first) & (key <= query), F32(0.0), F32(-1e30)
        )


def soft(len_ref, q_ref, do_ref, *refs):
    k_refs, dv_refs, stat_ref = refs[:5], refs[5:10], refs[10]
    q_rows, do_rows, bias, probs, keys = refs[11:]
    rows_of_heads(q_ref, q_rows)
    rows_of_heads(do_ref, do_rows)
    for slot, ref in enumerate(k_refs):
        keys[slot * TOK : (slot + 1) * TOK] = ref[...]
    fill_bias(len_ref, bias)
    for i in range(CHUNKS):
        cols = slice(i * LANES, (i + 1) * LANES)
        scores = lax.dot_general(keys[...], q_rows[cols], NT, preferred_element_type=F32)
        scores = scores * F32(SCALE) + bias[...]
        top = jnp.max(scores, axis=0, keepdims=True)
        weights = jnp.exp(scores - top)
        inverse = 1.0 / jnp.sum(weights, axis=0, keepdims=True)
        probs[:, cols] = (weights * inverse).astype(BF16)
        stat_ref[i : i + 1] = top
        stat_ref[CHUNKS + i : CHUNKS + i + 1] = inverse
    total = jnp.dot(probs[...], do_rows[...], preferred_element_type=F32)
    for slot, ref in enumerate(dv_refs):
        ref[...] = total[slot * TOK : (slot + 1) * TOK].astype(ref.dtype)


def attend(len_ref, q_ref, do_ref, stat_ref, *refs):
    k_refs, v_refs, (att_ref, dq_ref), dk_refs = refs[:5], refs[5:10], refs[10:12], refs[12:17]
    q_rows, do_rows, bias, dscores, keys, values = refs[17:]
    rows_of_heads(q_ref, q_rows)
    rows_of_heads(do_ref, do_rows)
    for slot in range(REACH + 1):
        keys[slot * TOK : (slot + 1) * TOK] = k_refs[slot][...]
        values[slot * TOK : (slot + 1) * TOK] = v_refs[slot][...]
    fill_bias(len_ref, bias)
    for i in range(CHUNKS):
        cols = slice(i * LANES, (i + 1) * LANES)
        scores = lax.dot_general(keys[...], q_rows[cols], NT, preferred_element_type=F32)
        scores = scores * F32(SCALE) + bias[...]
        p = jnp.exp(scores - stat_ref[i : i + 1]) * stat_ref[CHUNKS + i : CHUNKS + i + 1]
        att = lax.dot_general(values[...], p.astype(BF16), TN, preferred_element_type=F32)
        dp = lax.dot_general(values[...], do_rows[cols], NT, preferred_element_type=F32)
        dots = jnp.sum(p * dp, axis=0, keepdims=True)
        ds = (p * (dp - dots)).astype(BF16)
        dscores[:, cols] = ds
        dq = lax.dot_general(keys[...], ds, TN, preferred_element_type=F32) * F32(SCALE)
        att = att.T.astype(BF16)
        dq = dq.T.astype(BF16)
        for j in range(HEADS_AT_ONCE):
            head = slice((i * HEADS_AT_ONCE + j) * HEAD_DIM, (i * HEADS_AT_ONCE + j + 1) * HEAD_DIM)
            att_ref[:, head] = att[j * TOK : (j + 1) * TOK]
            dq_ref[:, head] = dq[j * TOK : (j + 1) * TOK]
    total = jnp.dot(dscores[...], q_rows[...], preferred_element_type=F32)
    for slot, ref in enumerate(dk_refs):
        ref[...] = total[slot * TOK : (slot + 1) * TOK].astype(ref.dtype)


def shards(queries, key_states, normed, value_weight, grad_out, lengths):
    yh, m1 = lax.axis_index("yh"), lax.axis_index("m1")
    corners = to_all(value_weight, ("yh", "m1"), 4)
    near = lax.ppermute(normed, "m0", PAIR)
    keys = [from_behind(key_states, d) for d in range(REACH, 0, -1)] + [key_states]
    corners, keys = lax.optimization_barrier((corners, keys))
    weight = to_all(lax.dynamic_slice_in_dim(corners, 2 * m1, 2, 0), "ctx", 8)
    heads = GROUP * TOK
    rows = pltpu.VMEM((heads, HEAD_DIM), BF16)
    window = pltpu.VMEM((WINDOW, HEAD_DIM), BF16)
    bias = pltpu.VMEM((WINDOW, LANES), F32)
    pairs = pltpu.VMEM((WINDOW, heads), BF16)
    block = shape((TOK, HEAD_DIM))
    own = shape((TOK, HEAD_DIM), F32)
    whole = shape((4, 8, 2, 64, HEAD_DIM))
    *dv, stats = call(
        soft, (block,) * REACH + (own, shape((8, LANES), F32)), 7, 3 * 10**9, 2 * 10**6,
        (rows, rows, bias, pairs, window), smem=1, vmem=28,
    )(lengths, queries, grad_out, *keys)
    weight, stats = lax.optimization_barrier((weight, stats))
    weight = to_all(weight, "x", 4)
    dv = [dv[REACH]] + [from_ahead(dv[REACH - d], d) for d in range(1, REACH + 1)]
    dv = sum_of(dv).astype(BF16)
    far_dv = lax.ppermute(dv, "m1", PAIR)
    other = lax.ppermute(weight, "core", PAIR)

    partial, given = call(weight_grad, (whole, whole), 4, 4 * 10**8, 5 * 10**6)(
        normed, near, dv, far_dv
    )
    taken = lax.ppermute(given, "core", PAIR)
    kept, given = call(project, (own, block), 4, 4 * 10**8, 5 * 10**6)(normed, near, weight, other)
    projected = (kept + lax.ppermute(given, "m1", PAIR).astype(F32)).astype(BF16)
    values = [from_behind(projected, d) for d in range(REACH, 0, -1)] + [projected]
    partial = call(add_halves, whole, 2, 10**6, 3 * 10**6)(partial, taken)
    partial = lax.all_to_all(partial, "x", 0, 0, tiled=True)
    partial = call(sum_blocks, shape((8, 2, 64, HEAD_DIM)), 1, 10**6, 10**6)(partial)
    partial, values = lax.optimization_barrier((partial, values))
    partial = lax.all_to_all(partial, "ctx", 0, 0, tiled=True)

    wide = shape((TOK, GROUP * HEAD_DIM))
    attended, grad_query, *dk = call(
        attend, (wide, wide) + (block,) * REACH + (own,), 13, 6 * 10**9, 4 * 10**6,
        (rows, rows, bias, pairs, window, window), smem=1, vmem=28,
    )(lengths, queries, grad_out, stats, *keys, *values)
    partial = call(twice_sum, shape((2, 2, 64, HEAD_DIM), F32), 1, 10**6, 10**6)(partial)
    partial, dk = lax.optimization_barrier((partial, dk))
    partial = lax.all_to_all(partial.reshape(4, 64, HEAD_DIM), ("yh", "m1"), 0, 0, tiled=True)
    grad_weight = jnp.sum(
        lax.dynamic_index_in_dim(
            partial.reshape(2, 2, 64, HEAD_DIM), yh, axis=1, keepdims=False
        ),
        axis=0,
    )
    dk = [dk[REACH]] + [from_ahead(dk[REACH - d], d) for d in range(1, REACH + 1)]
    grad_key = (sum(part.astype(F32) for part in dk) * F32(SCALE)).astype(BF16)
    return attended, grad_query, grad_key, grad_weight


def solution(mesh):
    axes = ("yh", "x", "core", "ctx", "m1", "m0")
    fine = Mesh(mesh.devices.reshape(2, 4, 2, 8, 2, 2), axes)
    tokens = P(axes[:4], axes[4:])
    return jax.shard_map(
        shards,
        mesh=fine,
        in_specs=(tokens,) * 5 + (P(axes[:3], None),),
        out_specs=(tokens,) * 4,
        check_vma=False,
    )
```

```python
import math

import jax
import jax.numpy as jnp
from jax import lax
from jax.experimental import pallas as pl
from jax.experimental.pallas import tpu as pltpu
from jax.sharding import Mesh, PartitionSpec as P

HEAD_DIM = 128
TOK = 192
GROUP = 8
REACH = 4
WINDOW = (REACH + 1) * TOK
HEADS_AT_ONCE = 2
LANES = HEADS_AT_ONCE * TOK
CHUNKS = GROUP // HEADS_AT_ONCE
PAIR = [(0, 1), (1, 0)]
SCALE = HEAD_DIM ** -0.5
LOG2_SCALE = SCALE * math.log2(math.e)
F32 = jnp.float32
BF16 = jnp.bfloat16
NT = (((1,), (1,)), ((), ()))
TN = (((0,), (0,)), ((), ()))
VMEM = pl.BlockSpec(memory_space=pltpu.VMEM)
SMEM = pl.BlockSpec(memory_space=pltpu.SMEM)


def shape(dims, dtype=BF16):
    return jax.ShapeDtypeStruct(dims, dtype)


def call(kernel, out_shape, n_in, flops, n_bytes, scratch=(), smem=0, vmem=20):
    outs = out_shape if isinstance(out_shape, tuple) else None
    return pl.pallas_call(
        kernel,
        out_shape=out_shape,
        in_specs=[SMEM] * smem + [VMEM] * n_in,
        out_specs=(VMEM,) * len(outs) if outs else VMEM,
        scratch_shapes=scratch,
        compiler_params=pltpu.CompilerParams(vmem_limit_bytes=vmem * 2**20),
        cost_estimate=pl.CostEstimate(
            flops=flops, bytes_accessed=n_bytes, transcendentals=0
        ),
        name=kernel.__name__,
    )


def to_all(block, axes, copies):
    return lax.all_to_all(
        jnp.broadcast_to(block[None], (copies,) + block.shape), axes, 0, 0, tiled=True
    )


def from_behind(block, distance):
    return lax.ppermute(block, "ctx", [(i, i + distance) for i in range(8 - distance)])


def from_ahead(block, distance):
    return lax.ppermute(block, "ctx", [(i + distance, i) for i in range(8 - distance)])


def feature_steps(own_ref, near_ref, half):
    m0 = lax.axis_index("m0")
    for step in range(4):
        ref, m = (own_ref, m0) if step < 2 else (near_ref, 1 - m0)
        place = pl.multiple_of((step % 2) * 1024 + half * 512, 512)
        yield ref[:, pl.ds(place, 512)], 2 * m + step % 2


def project(own_ref, near_ref, mine_ref, other_ref, keep_ref, give_ref):
    core, m1 = lax.axis_index("core"), lax.axis_index("m1")
    total = jnp.zeros((TOK, 2 * HEAD_DIM), F32)
    for w_ref, half in ((mine_ref, core), (other_ref, 1 - core)):
        for columns, x in feature_steps(own_ref, near_ref, half):
            weight = jnp.concatenate(
                [
                    jnp.concatenate([w_ref[x, ctx, c] for c in range(2)], axis=1)
                    for ctx in range(8)
                ],
                axis=0,
            )
            total += jnp.dot(columns, weight, preferred_element_type=F32)
    low, high = total[:, :HEAD_DIM], total[:, HEAD_DIM:]
    keep_ref[...] = jnp.where(m1 == 0, low, high)
    give_ref[...] = jnp.where(m1 == 0, high, low).astype(BF16)


def weight_grad(own_ref, near_ref, dv_ref, far_dv_ref, *out_refs):
    core, m1 = lax.axis_index("core"), lax.axis_index("m1")
    mine, far = dv_ref[...], far_dv_ref[...]
    dv = jnp.concatenate([jnp.where(m1 == 0, mine, far), jnp.where(m1 == 0, far, mine)], axis=1)
    for out_ref, half in zip(out_refs, (core, 1 - core)):
        for columns, x in feature_steps(own_ref, near_ref, half):
            rows = lax.dot_general(columns, dv, TN, preferred_element_type=F32).astype(BF16)
            for ctx in range(8):
                for c in range(2):
                    out_ref[x, c, ctx] = rows[
                        ctx * 64 : (ctx + 1) * 64, c * HEAD_DIM : (c + 1) * HEAD_DIM
                    ]


def add_halves(a_ref, b_ref, out_ref):
    out_ref[...] = (a_ref[...].astype(F32) + b_ref[...].astype(F32)).astype(BF16)


def sum_of(parts):
    total = parts[0].astype(F32)
    for part in parts[1:]:
        total = total + part.astype(F32)
    return total


def last_sum(parts_ref, out_ref):
    yh = lax.axis_index("yh")
    out_ref[...] = sum_of([parts_ref[i, yh, ctx] for i in range(2) for ctx in range(8)])


def twice_sum(parts_ref, out_ref):
    total = sum_of([parts_ref[i] for i in range(4)]).astype(BF16)
    for i in range(2):
        out_ref[i] = total


def rows_of_heads(wide_ref, rows_ref):
    for h in range(GROUP):
        rows_ref[h * TOK : (h + 1) * TOK] = wide_ref[:, h * HEAD_DIM : (h + 1) * HEAD_DIM]


def slot_owner(slot):
    return lax.rem(lax.axis_index("ctx") - (REACH - slot) + 8, 8)


def fill_bias(len_ref, bias):
    ctx = lax.axis_index("ctx")
    lane = lax.broadcasted_iota(jnp.int32, (1, LANES), 1)
    query = ctx * TOK + lax.rem(lane, TOK)
    first = jnp.zeros_like(query)
    end = jnp.int32(0)
    for d in range(8):
        end = end + len_ref[0, d]
        first = jnp.where(query >= end, end, first)
    offset = lax.broadcasted_iota(jnp.int32, (TOK, LANES), 0)
    for slot in range(REACH + 1):
        key = slot_owner(slot) * TOK + offset
        bias[slot * TOK : (slot + 1) * TOK] = jnp.where(
            (key >= first) & (key <= query), F32(0.0), F32(-1e30)
        )


def soft(len_ref, q_ref, do_ref, *refs):
    k_refs, dv_refs, stat_ref = refs[:5], refs[5:10], refs[10]
    q_rows, do_rows, bias, probs, keys = refs[11:]
    rows_of_heads(q_ref, q_rows)
    rows_of_heads(do_ref, do_rows)
    for slot, ref in enumerate(k_refs):
        keys[slot * TOK : (slot + 1) * TOK] = ref[...]
    fill_bias(len_ref, bias)
    for i in range(CHUNKS):
        cols = slice(i * LANES, (i + 1) * LANES)
        scores = lax.dot_general(keys[...], q_rows[cols], NT, preferred_element_type=F32)
        scores = scores * F32(LOG2_SCALE) + bias[...]
        top = jnp.max(scores, axis=0, keepdims=True)
        weights = jnp.exp2(scores - top)
        total = jnp.sum(weights, axis=0, keepdims=True)
        probs[:, cols] = (weights * (1.0 / total)).astype(BF16)
        stat_ref[i : i + 1] = top + jnp.log2(total)
    total = jnp.dot(probs[...], do_rows[...], preferred_element_type=F32)
    for slot, ref in enumerate(dv_refs):
        ref[...] = total[slot * TOK : (slot + 1) * TOK].astype(ref.dtype)


def attend(len_ref, q_ref, do_ref, stat_ref, *refs):
    k_refs, v_refs, (att_ref, dq_ref), dk_refs = refs[:5], refs[5:10], refs[10:12], refs[12:17]
    q_rows, do_rows, bias, dscores, keys, values = refs[17:]
    rows_of_heads(q_ref, q_rows)
    rows_of_heads(do_ref, do_rows)
    for slot in range(REACH + 1):
        keys[slot * TOK : (slot + 1) * TOK] = k_refs[slot][...]
        values[slot * TOK : (slot + 1) * TOK] = v_refs[slot][...]
    fill_bias(len_ref, bias)
    for i in range(CHUNKS):
        cols = slice(i * LANES, (i + 1) * LANES)
        scores = lax.dot_general(keys[...], q_rows[cols], NT, preferred_element_type=F32)
        scores = scores * F32(LOG2_SCALE) + bias[...]
        p = jnp.exp2(scores - stat_ref[i : i + 1])
        att = lax.dot_general(values[...], p.astype(BF16), TN, preferred_element_type=F32)
        dp = lax.dot_general(values[...], do_rows[cols], NT, preferred_element_type=F32)
        dots = jnp.sum(p * dp, axis=0, keepdims=True)
        ds = (p * (dp - dots)).astype(BF16)
        dscores[:, cols] = ds
        dq = lax.dot_general(keys[...], ds, TN, preferred_element_type=F32) * F32(SCALE)
        att = att.T.astype(BF16)
        dq = dq.T.astype(BF16)
        for j in range(HEADS_AT_ONCE):
            head = slice((i * HEADS_AT_ONCE + j) * HEAD_DIM, (i * HEADS_AT_ONCE + j + 1) * HEAD_DIM)
            att_ref[:, head] = att[j * TOK : (j + 1) * TOK]
            dq_ref[:, head] = dq[j * TOK : (j + 1) * TOK]
    total = jnp.dot(dscores[...], q_rows[...], preferred_element_type=F32)
    for slot, ref in enumerate(dk_refs):
        ref[...] = total[slot * TOK : (slot + 1) * TOK].astype(ref.dtype)


def shards(queries, key_states, normed, value_weight, grad_out, lengths):
    m1 = lax.axis_index("m1")
    corners = to_all(value_weight, ("yh", "m1"), 4)
    near = lax.ppermute(normed, "m0", PAIR)
    keys = [from_behind(key_states, d) for d in range(REACH, 0, -1)] + [key_states]
    corners, keys = lax.optimization_barrier((corners, keys))
    weight = to_all(lax.dynamic_slice_in_dim(corners, 2 * m1, 2, 0), "ctx", 8)
    heads = GROUP * TOK
    rows = pltpu.VMEM((heads, HEAD_DIM), BF16)
    window = pltpu.VMEM((WINDOW, HEAD_DIM), BF16)
    bias = pltpu.VMEM((WINDOW, LANES), F32)
    pairs = pltpu.VMEM((WINDOW, heads), BF16)
    block = shape((TOK, HEAD_DIM))
    own = shape((TOK, HEAD_DIM), F32)
    whole = shape((4, 2, 8, 64, HEAD_DIM))
    *dv, stats = call(
        soft, (block,) * REACH + (own, shape((8, LANES), F32)), 7, 3 * 10**9, 2 * 10**6,
        (rows, rows, bias, pairs, window), smem=1, vmem=28,
    )(lengths, queries, grad_out, *keys)
    weight, stats = lax.optimization_barrier((weight, stats))
    weight = to_all(weight, "x", 4)
    dv = [dv[REACH]] + [from_ahead(dv[REACH - d], d) for d in range(1, REACH + 1)]
    dv = sum_of(dv).astype(BF16)
    far_dv = lax.ppermute(dv, "m1", PAIR)
    other = lax.ppermute(weight, "core", PAIR)

    partial, given = call(weight_grad, (whole, whole), 4, 4 * 10**8, 5 * 10**6)(
        normed, near, dv, far_dv
    )
    taken = lax.ppermute(given, "core", PAIR)
    kept, given = call(project, (own, block), 4, 4 * 10**8, 5 * 10**6)(normed, near, weight, other)
    projected = (kept + lax.ppermute(given, "m1", PAIR).astype(F32)).astype(BF16)
    values = [from_behind(projected, d) for d in range(REACH, 0, -1)] + [projected]
    partial = call(add_halves, whole, 2, 10**6, 3 * 10**6)(partial, taken)
    partial = lax.all_to_all(partial, "x", 0, 0, tiled=True)
    partial = call(twice_sum, shape((2, 2, 8, 64, HEAD_DIM)), 1, 10**6, 10**6)(partial)
    partial, values = lax.optimization_barrier((partial, values))
    partial = lax.all_to_all(
        partial.reshape(32, 64, HEAD_DIM), ("yh", "m1", "ctx"), 0, 0, tiled=True
    )

    wide = shape((TOK, GROUP * HEAD_DIM))
    attended, grad_query, *dk = call(
        attend, (wide, wide) + (block,) * REACH + (own,), 13, 6 * 10**9, 4 * 10**6,
        (rows, rows, bias, pairs, window, window), smem=1, vmem=28,
    )(lengths, queries, grad_out, stats, *keys, *values)
    dk = [dk[REACH]] + [from_ahead(dk[REACH - d], d) for d in range(1, REACH + 1)]
    grad_key = (sum(part.astype(F32) for part in dk) * F32(SCALE)).astype(BF16)
    grad_weight = call(last_sum, shape((64, HEAD_DIM), F32), 1, 10**6, 10**6)(
        partial.reshape(2, 2, 8, 64, HEAD_DIM)
    )
    return attended, grad_query, grad_key, grad_weight


def solution(mesh):
    axes = ("yh", "x", "core", "ctx", "m1", "m0")
    fine = Mesh(mesh.devices.reshape(2, 4, 2, 8, 2, 2), axes)
    tokens = P(axes[:4], axes[4:])
    return jax.shard_map(
        shards,
        mesh=fine,
        in_specs=(tokens,) * 5 + (P(axes[:3], None),),
        out_specs=(tokens,) * 4,
        check_vma=False,
    )
```
